128 devices in a mesh: wide: 16 (over z_hi, x, core), narrow: 8 (over z_lo, y).
Axes of the slice: x: 4, y: 4, z: 4 (z_hi: 2, z_lo: 2; z = z_hi * 2 + z_lo), core: 2. Of those that a mesh axis runs over, the one named last changes fastest.
Arguments:
- populations: float32 [19, 4, 1024, 2048], P(None, None, ('wide', 'narrow')), as said below
- phase: int32 [4, 1024, 2048], P(None, ('wide', 'narrow')), may hold values from 0 to 2, as said below
- porosity: float32 [4, 1024, 2048], P(None, ('wide', 'narrow')), may hold values from 0 to 1, as said below
- napl: float32 [4, 1024, 2048], P(None, ('wide', 'narrow')), may hold values from 0 to 0.9, as said below
- concentration: float32 [4, 1024, 2048], P(None, ('wide', 'narrow')), may hold values from 0 to 1
- flags: int32 [2, 4, 2048], replicated, may hold values 0 or 1
Outputs:
- populations_out: float32 [19, 4, 1024, 2048], P(None, None, ('wide', 'narrow'))
- concentration_out: float32 [4, 1024, 2048], P(None, 'wide', 'narrow')
- napl_out: float32 [4, 1024, 2048], P(None, 'wide', 'narrow')
The draws below stay inside these ranges and needn't reach their ends.
Inputs may be any that keep to these rules, and one draw needn't show every extreme that they name: `phase`: 0 open pore, 1 pore holding NAPL, 2 solid. `porosity`: exactly 0 on voxels of phase 2 and 0.35 or more elsewhere. `napl`: above 0 exactly on voxels of phase 1, 0 elsewhere. `populations`: every entry positive.
All inputs are finite; a program needn't handle non-finite values.
Results may differ from the reference program's by a relative error of at most 0.0003.
Values sent between devices are 32-bit elements; how exact they have to be, the bound alone decides.
A program may use at most 128 MiB of HBM per device.

```python
import jax
import jax.numpy as jnp
import numpy as np
from jax import lax

Z = 4
LBM_STEPS = 4
TVD_STEPS = 2
X = 1024
Y = 2048


lattice_dirs = np.array([[0, 0, 0], [1, 0, 0], [-1, 0, 0], [0, 1, 0], [0, -1, 0], [0, 0, 1], [0, 0, -1], [1, 1, 0], [-1, -1, 0], [1, -1, 0], [-1, 1, 0], [1, 0, 1], [-1, 0, -1], [1, 0, -1], [-1, 0, 1], [0, 1, 1], [0, -1, -1], [0, 1, -1], [0, -1, 1]])


lattice_weights = np.array([1.0 / 3.0] + [1.0 / 18.0] * 6 + [1.0 / 36.0] * 12)


def phase_labels(key):
    scores = jax.random.randint(jax.random.fold_in(key, 5), (Z, X, Y), 0, 100)
    return jnp.where(scores < 30, 2, jnp.where(scores < 45, 1, 0)).astype(jnp.int32)


def draw_phase(key, part):
    return phase_labels(key)


def draw_porosity(key, part):
    labels = phase_labels(key)
    spread = jax.random.uniform(jax.random.fold_in(key, 6), (Z, X, Y), jnp.float32)
    return jnp.where(labels == 2, 0.0, 0.35 + 0.65 * spread).astype(jnp.float32)


def draw_napl(key, part):
    labels = phase_labels(key)
    spread = jax.random.uniform(jax.random.fold_in(key, 7), (Z, X, Y), jnp.float32)
    return jnp.where(labels == 1, 0.2 + 0.7 * spread, 0.0).astype(jnp.float32)


def draw_populations(key, part):
    density = jax.random.uniform(jax.random.fold_in(key, 8), (Z, X, Y), jnp.float32, 0.9, 1.1)
    velocity = jax.random.uniform(jax.random.fold_in(key, 9), (3, Z, X, Y), jnp.float32, -0.12, 0.12)
    jitter = jax.random.uniform(jax.random.fold_in(key, 10), (19, Z, X, Y), jnp.float32, 0.85, 1.15)
    planes = []
    for direction in range(19):
        layer_c = float(lattice_dirs[direction][2])
        flow_c = float(lattice_dirs[direction][0])
        cross_c = float(lattice_dirs[direction][1])
        proj = layer_c * velocity[0] + flow_c * velocity[1] + cross_c * velocity[2]
        planes.append(float(lattice_weights[direction]) * density * (1.0 + 3.0 * proj))
    return (jnp.stack(planes) * jitter).astype(jnp.float32)


def set_ends(drawn, key, smallest, largest):
    shape = drawn.shape
    place = [jax.random.randint(jax.random.fold_in(key, axis), (), 0, shape[axis]) for axis in range(len(shape))]
    drawn = drawn.at[tuple(place)].set(smallest)
    longest = shape.index(max(shape))
    place[longest] = (place[longest] + 1) % shape[longest]
    return drawn.at[tuple(place)].set(largest)


def block_scale(stream_key, shape, split, smallest, top_value):
    def one(axis_at, blocks):
        draws = jax.random.uniform(jax.random.fold_in(jax.random.fold_in(stream_key, 6), axis_at), (blocks,), jnp.float32, smallest / len(split), top_value / len(split))
        return jnp.repeat(jnp.exp(draws), shape[axis_at] // blocks).reshape((-1,) + (1,) * (len(shape) - axis_at - 1))

    level = one(*split[0])
    for cut in split[1:]:
        level = level * one(*cut)
    return level


def setup_inputs(seed: int = 0) -> dict:
    arg_keys = jax.random.split(jax.random.key(seed), 7)
    return {
        "populations": draw_populations(jax.random.fold_in(arg_keys[6], 71), 0),
        "phase": draw_phase(jax.random.fold_in(arg_keys[6], 71), 0),
        "porosity": draw_porosity(jax.random.fold_in(arg_keys[6], 71), 0),
        "napl": draw_napl(jax.random.fold_in(arg_keys[6], 71), 0),
        "concentration": jnp.clip(1.0 * jax.random.uniform(arg_keys[4], (Z, X, Y), jnp.float32) ** block_scale(arg_keys[4], (Z, X, Y), ((1, 128),), -0.2, 0.2), 0.0, 1.0),
        "flags": set_ends((jax.random.randint(arg_keys[5], (2, Z, Y), 0, 2) < 1).astype(jnp.int32), jax.random.fold_in(arg_keys[5], 1), 0, 1),
    }


lattice_dirs = np.array([[0, 0, 0], [1, 0, 0], [-1, 0, 0], [0, 1, 0], [0, -1, 0], [0, 0, 1], [0, 0, -1],
                         [1, 1, 0], [-1, -1, 0], [1, -1, 0], [-1, 1, 0], [1, 0, 1], [-1, 0, -1], [1, 0, -1],
                         [-1, 0, 1], [0, 1, 1], [0, -1, -1], [0, 1, -1], [0, -1, 1]])
lattice_weights = np.array([1.0 / 3.0] + [1.0 / 18.0] * 6 + [1.0 / 36.0] * 12)
opposite_dir = [0, 2, 1, 4, 3, 6, 5, 8, 7, 10, 9, 12, 11, 14, 13, 16, 15, 18, 17]
relax_time = 0.8
napl_drag = 0.5
diffusion = 0.15
transfer = 0.3
depletion = 0.5
porosity_floor = 0.3


def moments(popul):
    dirs = jnp.asarray(lattice_dirs.T, jnp.float32)
    return jnp.einsum('kq,qzxy->kzxy', dirs, popul, precision=lax.Precision.HIGHEST)


def collide(popul, phase):
    density = jnp.sum(popul, axis=0)
    moment = moments(popul)
    factor = jnp.where(phase == 1, napl_drag, 1.0)
    velocity = moment / density[None] * factor[None]
    dirs = jnp.asarray(lattice_dirs, jnp.float32)
    proj = jnp.einsum('qk,kzxy->qzxy', dirs, velocity, precision=lax.Precision.HIGHEST)
    square = jnp.sum(velocity * velocity, axis=0)
    weights = jnp.asarray(lattice_weights, jnp.float32)[:, None, None, None]
    equil = weights * density[None] * (1.0 + 3.0 * proj + 4.5 * proj * proj - 1.5 * square[None])
    return popul - (popul - equil) / relax_time


def shift_cells(field, offset, fill):
    if offset == 0:
        return field
    edge = jnp.full(field.shape[:-1] + (1,), fill, field.dtype)
    if offset > 0:
        return jnp.concatenate([edge, field[..., :-1]], axis=-1)
    return jnp.concatenate([field[..., 1:], edge], axis=-1)


def minmod(left, right):
    return 0.5 * (jnp.sign(left) + jnp.sign(right)) * jnp.minimum(jnp.abs(left), jnp.abs(right))


def face_balance(conc_pad, poro_pad, vel_pad, along, extent):
    def layer_at(field, start):
        return lax.slice_in_dim(field, start, start + extent + 1, axis=along)
    conc_back = layer_at(conc_pad, 0)
    conc_here = layer_at(conc_pad, 1)
    conc_next = layer_at(conc_pad, 2)
    conc_far = layer_at(conc_pad, 3)
    open_face = layer_at(poro_pad, 1) * layer_at(poro_pad, 2)
    carried = open_face * 0.5 * (layer_at(vel_pad, 1) + layer_at(vel_pad, 2))
    upwind = conc_here + 0.5 * minmod(conc_here - conc_back, conc_next - conc_here)
    downwind = conc_next - 0.5 * minmod(conc_next - conc_here, conc_far - conc_next)
    flux = carried * jnp.where(carried > 0, upwind, downwind) - diffusion * open_face * (conc_next - conc_here)
    return lax.slice_in_dim(flux, 0, extent, axis=along) - lax.slice_in_dim(flux, 1, extent + 1, axis=along)


def pad_ends(field, low_rows, high_rows):
    return jnp.concatenate([low_rows, low_rows, field, high_rows, high_rows], axis=-2)


def pad_side(field):
    return jnp.pad(field, ((0, 0), (0, 0), (2, 2)))


def wrap_layers(field):
    return jnp.concatenate([field[-2:], field, field[:2]], axis=0)


def reference(populations, phase, porosity, napl, concentration, flags):
    solid = phase == 2
    popul = populations
    for _ in range(LBM_STEPS):
        post = collide(popul, phase)
        moved_all = []
        for direction in range(19):
            x_step = int(lattice_dirs[direction][0])
            y_step = int(lattice_dirs[direction][1])
            z_step = int(lattice_dirs[direction][2])
            moved = jnp.roll(post[direction], x_step, axis=1)
            moved = jnp.roll(shift_cells(moved, y_step, 0.0), z_step, axis=0)
            source = jnp.roll(solid, x_step, axis=1)
            source = jnp.roll(shift_cells(source, y_step, True), z_step, axis=0)
            bounced = jnp.where(source, post[opposite_dir[direction]], moved)
            moved_all.append(jnp.where(solid, popul[direction], bounced))
        popul = jnp.stack(moved_all)
    density = jnp.sum(popul, axis=0)
    momentum = jnp.where(solid[None], 0.0, moments(popul) / density[None])
    velocity = jnp.stack([momentum[2], momentum[0], momentum[1]])
    flag_rows = flags.astype(jnp.float32)
    poro_x = pad_ends(porosity, flag_rows[0][:, None, :], flag_rows[1][:, None, :])
    xvel_x = pad_ends(velocity[1], velocity[1][:, :1, :], velocity[1][:, -1:, :])
    poro_y = pad_side(porosity)
    yvel_y = pad_side(velocity[2])
    poro_z = wrap_layers(porosity)
    zvel_z = wrap_layers(velocity[0])
    conc = concentration
    remain = napl
    for _ in range(TVD_STEPS):
        conc_x = pad_ends(conc, jnp.zeros_like(conc[:, :1, :]), conc[:, -1:, :])
        change = face_balance(conc_x, poro_x, xvel_x, 1, conc.shape[1])
        change = change + face_balance(pad_side(conc), poro_y, yvel_y, 2, conc.shape[2])
        change = change + face_balance(wrap_layers(conc), poro_z, zvel_z, 0, conc.shape[0])
        rate = transfer * remain * (1.0 - conc)
        conc = conc + (change + rate) / jnp.maximum(porosity, porosity_floor)
        remain = remain - depletion * rate
    return popul, conc, remain
```

```python
import functools

import jax
import jax.numpy as jnp
from jax import lax
from jax.experimental import pallas as pl
from jax.experimental.pallas import tpu as pltpu
from jax.sharding import PartitionSpec as P

MESH = pl.DeviceIdType.MESH
DIRS = [
    (0, 0, 0), (1, 0, 0), (-1, 0, 0), (0, 1, 0), (0, -1, 0), (0, 0, 1), (0, 0, -1),
    (1, 1, 0), (-1, -1, 0), (1, -1, 0), (-1, 1, 0), (1, 0, 1), (-1, 0, -1), (1, 0, -1), (-1, 0, 1),
    (0, 1, 1), (0, -1, -1), (0, 1, -1), (0, -1, 1),
]
OPP = [0, 2, 1, 4, 3, 6, 5, 8, 7, 10, 9, 12, 11, 14, 13, 16, 15, 18, 17]
UP = [1, 7, 9, 11, 13]
DOWN = [2, 8, 10, 12, 14]
ORDER = UP + DOWN + [0, 3, 4, 5, 6, 15, 16, 17, 18]
SLOT = {q: i for i, q in enumerate(ORDER)}
STEPS = 4
Z = 4
R = 8
B = 128


def collide(f, phase):
    total, diff = {}, {}
    for q in range(1, 19, 2):
        total[q] = f[q] + f[q + 1]
        diff[q] = f[q] - f[q + 1]
    rho = (
        ((f[0] + total[1]) + (total[3] + total[5]))
        + ((total[7] + total[9]) + (total[11] + total[13]))
        + (total[15] + total[17])
    )
    jx = (diff[1] + diff[7]) + (diff[9] + diff[11]) + diff[13]
    jy = (diff[3] + diff[7]) + (diff[15] - diff[9]) + diff[17]
    jz = (diff[5] + diff[11]) + (diff[15] - diff[13]) - diff[17]
    rho = jnp.where(phase == 2, jnp.nan, rho)
    factor = jnp.where(phase == 1, 0.5, 1.0)
    per = factor / rho
    vx, vy, vz = jx * per, jy * per, jz * per
    factor = factor * (3.75 / 36.0)
    nx, ny, nz = jx * factor, jy * factor, jz * factor
    hx, hy, hz = vx * 1.5, vy * 1.5, vz * 1.5
    sxx, syy, szz = nx * hx, ny * hy, nz * hz
    hx, hy = hx + hx, hy + hy
    xy, xz, yz = ny * hx, nz * hx, nz * hy
    even = rho * (1.25 / 36.0) - (sxx + syy + szz) * (1.0 / 3.0)
    post = [None] * 19
    post[0] = 12.0 * even - 0.25 * f[0]

    def pair(q, e, o):
        post[q] = (e + o) - 0.25 * f[q]
        post[q + 1] = (e - o) - 0.25 * f[q + 1]

    ex, ey, ez = even + sxx, even + syy, even + szz
    pair(1, ex + ex, nx + nx)
    pair(3, ey + ey, ny + ny)
    pair(5, ez + ez, nz + nz)
    exy, exz, eyz = ex + syy, ex + szz, ey + szz
    pair(7, exy + xy, nx + ny)
    pair(9, exy - xy, nx - ny)
    pair(11, exz + xz, nx + nz)
    pair(13, exz - xz, nx - nz)
    pair(15, eyz + yz, ny + nz)
    pair(17, eyz - yz, ny - nz)
    return post


def moments(f):
    total, diff = {}, {}
    for q in range(1, 19, 2):
        total[q] = f[q] + f[q + 1]
        diff[q] = f[q] - f[q + 1]
    rho = (
        ((f[0] + total[1]) + (total[3] + total[5]))
        + ((total[7] + total[9]) + (total[11] + total[13]))
        + (total[15] + total[17])
    )
    jx = (diff[1] + diff[7]) + (diff[9] + diff[11]) + diff[13]
    jy = (diff[3] + diff[7]) + (diff[15] - diff[9]) + diff[17]
    jz = (diff[5] + diff[11]) + (diff[15] - diff[13]) - diff[17]
    return rho, jx, jy, jz


def half_minmod(p, q):
    return 0.5 * jnp.maximum(jnp.minimum(p, q), jnp.minimum(jnp.maximum(p, q), 0.0))


def face_flux(back, here, ahead, far, w, a):
    step = ahead - here
    up = here + half_minmod(here - back, step)
    down = ahead - half_minmod(step, far - ahead)
    return a * jnp.where(a > 0, up, down) - (0.15 * w) * step


def body(
    wide, narrow, width, tile,
    pop_in, phase_in, poro_in, napl_in, conc_in, flags_in,
    pop_out, conc_out, napl_out,
    fbuf, phase, poro, napl, conc, conc2, flags, post, lo, hi,
    plo, phi, clo, chi, ulo, uhi, ux, uy, uz, wx, wl, wy, wz, ax, al, ay, az, inv,
    load_sem, small_sem, out_sem, own_sem,
    send_sem, recv_sem, psend, precv, csend, crecv, usend, urecv, asend, arecv,
):
    w, n = lax.axis_index("wide"), lax.axis_index("narrow")
    chunks = narrow
    per_chunk = tile // B
    strip = w * narrow + n

    def neighbour(offset):
        g = lax.rem(strip + offset + wide * narrow, wide * narrow)
        return (g // narrow, lax.rem(g, narrow))

    after, before = neighbour(1), neighbour(-1)
    first, last = strip == 0, strip == wide * narrow - 1

    def cols(k):
        return pl.ds(pl.multiple_of(k * tile, tile), tile)

    def pcols(k):
        return pl.ds(pl.multiple_of(B + k * tile, B), tile)

    def load(k):
        return pltpu.make_async_copy(
            pop_in.at[:, :, :, cols(k)], fbuf.at[:, :, :, cols(k)], load_sem.at[k]
        )

    smalls = [
        pltpu.make_async_copy(phase_in, phase, small_sem.at[0]),
        pltpu.make_async_copy(poro_in, poro.at[:, :, pl.ds(B, width)], small_sem.at[1]),
        pltpu.make_async_copy(conc_in, conc.at[0, :, :, pl.ds(B, width)], small_sem.at[2]),
        pltpu.make_async_copy(napl_in, napl, small_sem.at[3]),
        pltpu.make_async_copy(flags_in, flags, small_sem.at[4]),
    ]
    smalls[0].start()
    load(0).start()
    for copy in smalls[1:]:
        copy.start()
    for k in range(1, chunks):
        load(k).start()

    barrier = pltpu.get_barrier_semaphore()
    pl.semaphore_signal(barrier, inc=1, device_id=after, device_id_type=MESH)
    pl.semaphore_signal(barrier, inc=1, device_id=before, device_id_type=MESH)
    for k in range(1, narrow):
        pl.semaphore_signal(
            barrier, inc=1, device_id=(w, lax.rem(n + k, narrow)), device_id_type=MESH
        )

    lane = lax.broadcasted_iota(jnp.int32, (R, B), 1)
    row = lax.broadcasted_iota(jnp.int32, (R, B), 0)
    nan = jnp.full((R, B), jnp.nan, jnp.float32)
    zero = jnp.zeros((R, B), jnp.float32)
    ends = (pl.ds(0, B), pl.ds(B + width, B))

    def fill(z, carry):
        for end in ends:
            for p in range(2):
                for q in range(19):
                    if DIRS[q][1]:
                        post[p, SLOT[q], z, :, end] = nan
            for s in range(STEPS):
                for m in (1, 2):
                    lo[s, m, z, :, end] = nan
                    hi[s, m, z, :, end] = nan
            poro[z, :, end] = zero
            uy[z, :, end] = zero
            for p in range(2):
                conc[p, z, :, end] = zero
        return carry

    lax.fori_loop(0, Z, fill, 0)

    def edge(s, side, k):
        p = lax.rem(s, 2)
        if side == 0:
            src = post.at[p, pl.ds(0, 5), :, pl.ds(R - 1, 1), pcols(k)]
            dst = lo.at[s, :, :, pl.ds(R - 1, 1), pcols(k)]
        else:
            src = post.at[p, pl.ds(5, 5), :, pl.ds(0, 1), pcols(k)]
            dst = hi.at[s, :, :, pl.ds(0, 1), pcols(k)]
        return pltpu.make_async_remote_copy(
            src_ref=src, dst_ref=dst, send_sem=send_sem.at[s, side, k], recv_sem=recv_sem.at[s, side, k],
            device_id=after if side == 0 else before, device_id_type=MESH,
        )

    def poro_edge(side):
        rows = pl.ds(R - 1, 1) if side == 0 else pl.ds(0, 1)
        inner = pl.ds(B, width)
        return pltpu.make_async_remote_copy(
            src_ref=poro.at[:, rows, inner], dst_ref=(plo if side == 0 else phi).at[:, rows, :],
            send_sem=psend.at[side], recv_sem=precv.at[side],
            device_id=after if side == 0 else before, device_id_type=MESH,
        )

    def conc_edge(p, side, k):
        rows = pl.ds(R - 2, 2) if side == 0 else pl.ds(0, 2)
        return pltpu.make_async_remote_copy(
            src_ref=conc.at[p, :, rows, pcols(k)], dst_ref=(clo if side == 0 else chi).at[p, :, rows, cols(k)],
            send_sem=csend.at[p, side, k], recv_sem=crecv.at[p, side, k],
            device_id=after if side == 0 else before, device_id_type=MESH,
        )

    def vel_edge(side, k):
        rows = pl.ds(R - 1, 1) if side == 0 else pl.ds(0, 1)
        return pltpu.make_async_remote_copy(
            src_ref=ux.at[:, rows, cols(k)], dst_ref=(ulo if side == 0 else uhi).at[:, rows, cols(k)],
            send_sem=usend.at[side, k], recv_sem=urecv.at[side, k],
            device_id=after if side == 0 else before, device_id_type=MESH,
        )

    def to_tile(a, k):
        src, dst = (napl, napl_out) if a == 0 else (conc2, conc_out)
        rows = pl.ds(pl.multiple_of(n * R, R), R)
        return pltpu.make_async_remote_copy(
            src_ref=src.at[:, :, cols(k)], dst_ref=dst.at[:, rows, :],
            send_sem=asend.at[a, k], recv_sem=arecv.at[a, n], device_id=(w, k), device_id_type=MESH,
        )

    def from_tile(a, k):
        src, dst = (napl, napl_out) if a == 0 else (conc2, conc_out)
        rows = pl.ds(pl.multiple_of(k * R, R), R)
        return pltpu.make_async_remote_copy(
            src_ref=src.at[:, :, cols(k)], dst_ref=dst.at[:, rows, :],
            send_sem=asend.at[a, k], recv_sem=arecv.at[a, k], device_id=(w, k), device_id_type=MESH,
        )

    def own_tile(a):
        src, dst = (napl, napl_out) if a == 0 else (conc2, conc_out)
        rows = pl.ds(pl.multiple_of(n * R, R), R)
        return pltpu.make_async_copy(src.at[:, :, cols(n)], dst.at[:, rows, :], own_sem.at[a])

    def send_tile(a, k):
        @pl.when(k != n)
        def _():
            to_tile(a, k).start()

        @pl.when(k == n)
        def _():
            own_tile(a).start()

    def blocks(k, fn, carry=0):
        return lax.fori_loop(0, per_chunk, lambda i, c: fn(k * per_chunk + i, c), carry)

    def at(b):
        return pl.ds(pl.multiple_of(b * B, B), B)

    def start_block(b, carry):
        here, there = at(b), at(b + 1)
        for z in range(Z):
            f = [fbuf[q, z, :, here] for q in range(19)]
            out = collide(f, phase[z, :, here])
            for q in range(19):
                post[0, SLOT[q], z, :, there] = out[q]
        return carry

    smalls[0].wait()
    load(0).wait()
    blocks(0, start_block)
    pl.semaphore_wait(barrier, narrow + 1)
    for side in range(2):
        edge(0, side, 0).start()
    for copy in smalls[1:3]:
        copy.wait()
    for side in range(2):
        poro_edge(side).start()

    def first_chunk(k, carry):
        load(k).wait()
        blocks(k, start_block)
        for side in range(2):
            edge(0, side, k).start()
        return carry

    lax.fori_loop(1, chunks, first_chunk, 0)
    for side in range(2):
        for k in range(chunks):
            conc_edge(0, side, k).start()
    for copy in smalls[3:]:
        copy.wait()

    def stream(p, s, z, b):
        base = b * B + B

        def block(slot, layer, shift, ex):
            where = pl.ds(pl.multiple_of(base + shift, B), B)
            value = post[p, slot, layer, :, where]
            if ex == 1:
                value = jnp.where(row == R - 1, lo[s, slot, layer, :, where], value)
            elif ex == -1:
                value = jnp.where(row == 0, hi[s, slot - 5, layer, :, where], value)
            return value

        here = pl.ds(pl.multiple_of(base, B), B)
        f = []
        for q in range(19):
            ex, ey, ez = DIRS[q]
            slot, layer = SLOT[q], (z - ez) % Z
            if q == 0:
                f.append(post[p, slot, z, :, here])
                continue
            moved = block(slot, layer, 0, ex)
            if ey == 1:
                moved = pltpu.roll(jnp.where(lane == B - 1, block(slot, layer, -B, ex), moved), 1, 1)
            elif ey == -1:
                moved = pltpu.roll(jnp.where(lane == 0, block(slot, layer, B, ex), moved), B - 1, 1)
            if ex:
                moved = pltpu.roll(moved, 1 if ex == 1 else R - 1, 0)
            f.append(jnp.where(moved < jnp.inf, moved, post[p, SLOT[OPP[q]], z, :, here]))
        return f

    def await_edges(s, k):
        @pl.when(k == 0)
        def _():
            for side in range(2):
                edge(s, side, k).wait_recv()

        @pl.when(k < chunks - 1)
        def _():
            for side in range(2):
                edge(s, side, k + 1).wait_recv()

    def one_step(s, carry):
        old, new = lax.rem(s + 1, 2), lax.rem(s, 2)

        def move_block(b, c):
            for z in range(Z):
                out = collide(stream(old, s - 1, z, b), phase[z, :, at(b)])
                for q in range(19):
                    post[new, SLOT[q], z, :, at(b + 1)] = out[q]
            return c

        def chunk(k, c):
            await_edges(s - 1, k)

            @pl.when(s >= 2)
            def _():
                for side in range(2):
                    edge(s - 2, side, k).wait_send()

            blocks(k, move_block)
            for side in range(2):
                edge(s, side, k).start()
            return c

        lax.fori_loop(0, chunks, chunk, 0)

        @pl.when(s == 1)
        def _():
            for side in range(2):
                poro_edge(side).wait_recv()

            def coef(b, c):
                here, there, beyond = at(b), at(b + 1), at(b + 2)
                for z in range(Z):
                    own = poro[z, :, there]
                    high = jnp.where(last, flags[1, z : z + 1, here].astype(jnp.float32), phi[z, :, here])
                    low = jnp.where(first, flags[0, z : z + 1, here].astype(jnp.float32), plo[z, :, here])
                    wx[z, :, here] = own * pltpu.roll(jnp.where(row == 0, high, own), R - 1, 0)
                    wl[z, :, here] = low * pltpu.roll(own, R - 1, 0)
                    wy[z, :, here] = own * pltpu.roll(jnp.where(lane == 0, poro[z, :, beyond], own), B - 1, 1)
                    wz[z, :, here] = own * poro[(z + 1) % Z, :, there]
                    inv[z, :, here] = 1.0 / jnp.maximum(own, 0.3)
                return c

            lax.fori_loop(0, width // B, coef, 0)

        return carry

    lax.fori_loop(1, STEPS, one_step, 0)

    def last_block(b, carry):
        here, there = at(b), at(b + 1)
        for z in range(Z):
            f = stream((STEPS - 1) % 2, STEPS - 1, z, b)
            solid = phase[z, :, here] == 2
            rho, jx, jy, jz = moments(f)
            per = jnp.where(solid, 0.0, 1.0) / jnp.where(solid, 1.0, rho)
            ux[z, :, here] = jnp.where(solid, 0.0, jx * per)
            uy[z, :, there] = jnp.where(solid, 0.0, jy * per)
            uz[z, :, here] = jnp.where(solid, 0.0, jz * per)
            for q in range(19):
                fbuf[q, z, :, here] = jnp.where(solid, fbuf[q, z, :, here], f[q])
        return carry

    def store(k):
        return pltpu.make_async_copy(
            fbuf.at[:, :, :, cols(k)], pop_out.at[:, :, :, cols(k)], out_sem.at[k]
        )

    def last_chunk(k, carry):
        await_edges(STEPS - 1, k)
        blocks(k, last_block)
        for side in range(2):
            vel_edge(side, k).start()
        store(k).start()
        return carry

    lax.fori_loop(0, chunks, last_chunk, 0)

    def transport(step, b, carry):
        here, there, back, beyond = at(b), at(b + 1), at(b), at(b + 2)
        c = [conc[step, z, :, there] for z in range(Z)]
        if step == 0:
            for z in range(Z):
                vx = ux[z, :, here]
                high = jnp.where(last, pltpu.roll(vx, 1, 0), uhi[z, :, here])
                low = jnp.where(first, pltpu.roll(vx, R - 1, 0), ulo[z, :, here])
                nxt = pltpu.roll(vx, R - 1, 0)
                ax[z, :, here] = wx[z, :, here] * (0.5 * (vx + jnp.where(row == R - 1, pltpu.roll(high, R - 1, 0), nxt)))
                al[z, :, here] = wl[z, :, here] * (0.5 * (low + nxt))
                vy = uy[z, :, there]
                ay[z, :, here] = wy[z, :, here] * (
                    0.5 * (vy + pltpu.roll(jnp.where(lane == 0, uy[z, :, beyond], vy), B - 1, 1))
                )
                az[z, :, here] = wz[z, :, here] * (0.5 * (uz[z, :, here] + uz[(z + 1) % Z, :, here]))
        zflux = [
            face_flux(
                c[(z - 1) % Z], c[z], c[(z + 1) % Z], c[(z + 2) % Z], wz[z, :, here], az[z, :, here]
            )
            for z in range(Z)
        ]
        flow = []
        for z in range(Z):
            own = c[z]
            high = chi[step, z, :, here]
            low = clo[step, z, :, here]
            up1, up2 = pltpu.roll(own, R - 1, 0), pltpu.roll(own, R - 2, 0)
            low = jnp.where(first, 0.0, low)
            down1 = pltpu.roll(jnp.where(row == R - 1, low, own), 1, 0)
            end = pltpu.roll(own, 1, 0)
            one = jnp.where(last, end, high)
            two = jnp.where(last, jnp.where(row == 0, end, pltpu.roll(own, 2, 0)), high)
            ahead = pltpu.roll(jnp.where(row == 0, one, own), R - 1, 0)
            far = pltpu.roll(jnp.where(row < 2, two, own), R - 2, 0)
            xflux = face_flux(down1, own, ahead, far, wx[z, :, here], ax[z, :, here])
            xlow = face_flux(pltpu.roll(low, 1, 0), low, up1, up2, wl[z, :, here], al[z, :, here])
            change = pltpu.roll(jnp.where(row == R - 1, xlow, xflux), 1, 0) - xflux
            cb, cn = conc[step, z, :, back], conc[step, z, :, beyond]
            left = pltpu.roll(jnp.where(lane == B - 1, cb, own), 1, 1)
            right = pltpu.roll(jnp.where(lane == 0, cn, own), B - 1, 1)
            right2 = pltpu.roll(jnp.where(lane < 2, cn, own), B - 2, 1)
            yflux = face_flux(left, own, right, right2, wy[z, :, here], ay[z, :, here])
            flow.append(yflux)
            change = change + (pltpu.roll(jnp.where(lane == B - 1, carry[z], yflux), 1, 1) - yflux)
            change = change + (zflux[(z - 1) % Z] - zflux[z])
            s = napl[z, :, here]
            if step == 0:
                rate = 0.3 * s * (1.0 - own)
                new = own + (change + rate) * inv[z, :, here]
                conc[1, z, :, there] = new
                s = s - 0.5 * rate
                rate = 0.3 * s * (1.0 - new)
                napl[z, :, here] = s - 0.5 * rate
                conc2[z, :, here] = rate
            else:
                conc2[z, :, here] = own + (change + conc2[z, :, here]) * inv[z, :, here]
        return tuple(flow)

    def first_transport(k, carry):
        for side in range(2):
            vel_edge(side, k).wait_recv()
            conc_edge(0, side, k).wait_recv()
        carry = blocks(k, functools.partial(transport, 0), carry)
        for side in range(2):
            conc_edge(1, side, k).start()
        send_tile(0, k)
        return carry

    def second_transport(k, carry):
        for side in range(2):
            conc_edge(1, side, k).wait_recv()
        carry = blocks(k, functools.partial(transport, 1), carry)
        send_tile(1, k)
        return carry

    still = (zero,) * Z
    lax.fori_loop(0, chunks, first_transport, still)
    lax.fori_loop(0, chunks, second_transport, still)

    def settle(k, carry):
        for side in range(2):
            for s in (STEPS - 2, STEPS - 1):
                edge(s, side, k).wait_send()
            vel_edge(side, k).wait_send()
            for p in range(2):
                conc_edge(p, side, k).wait_send()
        store(k).wait()
        return carry

    lax.fori_loop(0, chunks, settle, 0)
    for side in range(2):
        poro_edge(side).wait_send()

    def settle_tile(k, carry):
        @pl.when(k != n)
        def _():
            for a in range(2):
                to_tile(a, k).wait_send()
                from_tile(a, k).wait_recv()

        return carry

    lax.fori_loop(0, chunks, settle_tile, 0)
    for a in range(2):
        own_tile(a).wait()


def local(wide, narrow, populations, phase, porosity, napl, concentration, flags):
    width = phase.shape[2]
    tile = width // narrow
    padded = width + 2 * B
    f32 = jnp.float32
    DMA = pltpu.SemaphoreType.DMA

    def full():
        return pltpu.VMEM((Z, R, width), f32)

    any_space = pl.BlockSpec(memory_space=pl.ANY)
    scratch = [
        pltpu.VMEM((19, Z, R, width), f32),
        pltpu.VMEM((Z, R, width), jnp.int32),
        pltpu.VMEM((Z, R, padded), f32),
        full(),
        pltpu.VMEM((2, Z, R, padded), f32),
        full(),
        pltpu.VMEM((2, Z, width), jnp.int32),
        pltpu.VMEM((2, 19, Z, R, padded), f32),
        pltpu.VMEM((STEPS, 5, Z, R, padded), f32),
        pltpu.VMEM((STEPS, 5, Z, R, padded), f32),
        full(), full(),
        pltpu.VMEM((2, Z, R, width), f32), pltpu.VMEM((2, Z, R, width), f32),
        full(), full(),
        full(), pltpu.VMEM((Z, R, padded), f32), full(),
        full(), full(), full(), full(),
        full(), full(), full(), full(),
        full(),
        DMA((narrow,)), DMA((5,)), DMA((narrow,)), DMA((2,)),
        DMA((STEPS, 2, narrow)), DMA((STEPS, 2, narrow)),
        DMA((2,)), DMA((2,)),
        DMA((2, 2, narrow)), DMA((2, 2, narrow)),
        DMA((2, narrow)), DMA((2, narrow)),
        DMA((2, narrow)), DMA((2, narrow)),
    ]
    tiles = jax.ShapeDtypeStruct((Z, R * narrow, tile), f32)
    return pl.pallas_call(
        functools.partial(body, wide, narrow, width, tile),
        out_shape=(jax.ShapeDtypeStruct(populations.shape, f32), tiles, tiles),
        in_specs=[any_space] * 6,
        out_specs=(any_space,) * 3,
        scratch_shapes=scratch,
        compiler_params=pltpu.CompilerParams(
            collective_id=0, has_side_effects=True, vmem_limit_bytes=56 * 2**20
        ),
        name="dissolution",
    )(populations, phase, porosity, napl, concentration, flags)


def solution(mesh):
    strips = ("wide", "narrow")
    in_specs = (
        P(None, None, strips, None),
        P(None, strips, None),
        P(None, strips, None),
        P(None, strips, None),
        P(None, strips, None),
        P(),
    )
    out_specs = (
        P(None, None, strips, None),
        P(None, "wide", "narrow"),
        P(None, "wide", "narrow"),
    )
    fn = functools.partial(local, mesh.shape["wide"], mesh.shape["narrow"])
    return jax.shard_map(fn, mesh=mesh, in_specs=in_specs, out_specs=out_specs, check_vma=False)
```

```python
import functools

import jax
import jax.numpy as jnp
from jax import lax
from jax.experimental import pallas as pl
from jax.experimental.pallas import tpu as pltpu
from jax.sharding import PartitionSpec as P

MESH = pl.DeviceIdType.MESH
DIRS = [
    (0, 0, 0), (1, 0, 0), (-1, 0, 0), (0, 1, 0), (0, -1, 0), (0, 0, 1), (0, 0, -1),
    (1, 1, 0), (-1, -1, 0), (1, -1, 0), (-1, 1, 0), (1, 0, 1), (-1, 0, -1), (1, 0, -1), (-1, 0, 1),
    (0, 1, 1), (0, -1, -1), (0, 1, -1), (0, -1, 1),
]
OPP = [0, 2, 1, 4, 3, 6, 5, 8, 7, 10, 9, 12, 11, 14, 13, 16, 15, 18, 17]
UP = [1, 7, 9, 11, 13]
DOWN = [2, 8, 10, 12, 14]
ORDER = UP + DOWN + [0, 3, 4, 5, 6, 15, 16, 17, 18]
SLOT = {q: i for i, q in enumerate(ORDER)}
STEPS = 4
Z = 4
R = 8
B = 128


def collide(f, phase):
    total, diff = {}, {}
    for q in range(1, 19, 2):
        total[q] = f[q] + f[q + 1]
        diff[q] = f[q] - f[q + 1]
    rho = (
        ((f[0] + total[1]) + (total[3] + total[5]))
        + ((total[7] + total[9]) + (total[11] + total[13]))
        + (total[15] + total[17])
    )
    jx = (diff[1] + diff[7]) + (diff[9] + diff[11]) + diff[13]
    jy = (diff[3] + diff[7]) + (diff[15] - diff[9]) + diff[17]
    jz = (diff[5] + diff[11]) + (diff[15] - diff[13]) - diff[17]
    rho = jnp.where(phase == 2, jnp.nan, rho)
    factor = jnp.where(phase == 1, 0.5, 1.0)
    per = factor / rho
    vx, vy, vz = jx * per, jy * per, jz * per
    factor = factor * (3.75 / 36.0)
    nx, ny, nz = jx * factor, jy * factor, jz * factor
    hx, hy, hz = vx * 1.5, vy * 1.5, vz * 1.5
    sxx, syy, szz = nx * hx, ny * hy, nz * hz
    hx, hy = hx + hx, hy + hy
    xy, xz, yz = ny * hx, nz * hx, nz * hy
    even = rho * (1.25 / 36.0) - (sxx + syy + szz) * (1.0 / 3.0)
    post = [None] * 19
    post[0] = 12.0 * even - 0.25 * f[0]

    def pair(q, e, o):
        post[q] = (e + o) - 0.25 * f[q]
        post[q + 1] = (e - o) - 0.25 * f[q + 1]

    ex, ey, ez = even + sxx, even + syy, even + szz
    pair(1, ex + ex, nx + nx)
    pair(3, ey + ey, ny + ny)
    pair(5, ez + ez, nz + nz)
    exy, exz, eyz = ex + syy, ex + szz, ey + szz
    pair(7, exy + xy, nx + ny)
    pair(9, exy - xy, nx - ny)
    pair(11, exz + xz, nx + nz)
    pair(13, exz - xz, nx - nz)
    pair(15, eyz + yz, ny + nz)
    pair(17, eyz - yz, ny - nz)
    return post


def moments(f):
    total, diff = {}, {}
    for q in range(1, 19, 2):
        total[q] = f[q] + f[q + 1]
        diff[q] = f[q] - f[q + 1]
    rho = (
        ((f[0] + total[1]) + (total[3] + total[5]))
        + ((total[7] + total[9]) + (total[11] + total[13]))
        + (total[15] + total[17])
    )
    jx = (diff[1] + diff[7]) + (diff[9] + diff[11]) + diff[13]
    jy = (diff[3] + diff[7]) + (diff[15] - diff[9]) + diff[17]
    jz = (diff[5] + diff[11]) + (diff[15] - diff[13]) - diff[17]
    return rho, jx, jy, jz


def half_minmod(p, q):
    return 0.5 * jnp.maximum(jnp.minimum(p, q), jnp.minimum(jnp.maximum(p, q), 0.0))


def face_flux(back, here, ahead, far, w, a):
    step = ahead - here
    up = here + half_minmod(here - back, step)
    down = ahead - half_minmod(step, far - ahead)
    return a * jnp.where(a > 0, up, down) - (0.15 * w) * step


def body(
    wide, narrow, width, tile,
    pop_in, phase_in, poro_in, napl_in, conc_in, flags_in,
    pop_out, conc_out, napl_out,
    fbuf, phase, poro, napl, conc0, conc1, conc2, rate_buf, flags, post0, post1, lo, hi,
    plo, phi, clo, chi, ulo, uhi, ux, uy, uz, wx, wl, wy, wz, ax, al, ay, az, inv,
    load_sem, small_sem, out_sem, own_sem,
    send_sem, recv_sem, psend, precv, csend, crecv, usend, urecv, asend, arecv,
):
    posts, concs = (post0, post1), (conc0, conc1)
    w, n = lax.axis_index("wide"), lax.axis_index("narrow")
    chunks = narrow
    per_chunk = tile // B
    strip = w * narrow + n

    def neighbour(offset):
        g = lax.rem(strip + offset + wide * narrow, wide * narrow)
        return (g // narrow, lax.rem(g, narrow))

    after, before = neighbour(1), neighbour(-1)
    first, last = strip == 0, strip == wide * narrow - 1

    def cols(k):
        return pl.ds(pl.multiple_of(k * tile, tile), tile)

    def pcols(k):
        return pl.ds(pl.multiple_of(B + k * tile, B), tile)

    def load(k):
        return pltpu.make_async_copy(
            pop_in.at[:, :, :, cols(k)], fbuf.at[:, :, :, cols(k)], load_sem.at[k]
        )

    smalls = [
        pltpu.make_async_copy(phase_in, phase, small_sem.at[0]),
        pltpu.make_async_copy(poro_in, poro.at[:, :, pl.ds(B, width)], small_sem.at[1]),
        pltpu.make_async_copy(conc_in, conc0.at[:, :, pl.ds(B, width)], small_sem.at[2]),
        pltpu.make_async_copy(napl_in, napl, small_sem.at[3]),
        pltpu.make_async_copy(flags_in, flags, small_sem.at[4]),
    ]
    smalls[0].start()
    load(0).start()
    for copy in smalls[1:]:
        copy.start()
    for k in range(1, chunks):
        load(k).start()

    barrier = pltpu.get_barrier_semaphore()
    pl.semaphore_signal(barrier, inc=1, device_id=after, device_id_type=MESH)
    pl.semaphore_signal(barrier, inc=1, device_id=before, device_id_type=MESH)
    for k in range(1, narrow):
        pl.semaphore_signal(
            barrier, inc=1, device_id=(w, lax.rem(n + k, narrow)), device_id_type=MESH
        )

    lane = lax.broadcasted_iota(jnp.int32, (R, B), 1)
    row = lax.broadcasted_iota(jnp.int32, (R, B), 0)
    nan = jnp.full((R, B), jnp.nan, jnp.float32)
    zero = jnp.zeros((R, B), jnp.float32)
    ends = (pl.ds(0, B), pl.ds(B + width, B))

    def fill(z, carry):
        for end in ends:
            for p in range(2):
                for q in range(19):
                    if DIRS[q][1]:
                        posts[p][SLOT[q], z, :, end] = nan
            for s in range(STEPS):
                for m in (1, 2):
                    lo[s, m, z, :, end] = nan
                    hi[s, m, z, :, end] = nan
            poro[z, :, end] = zero
            uy[z, :, end] = zero
            for p in range(2):
                concs[p][z, :, end] = zero
        return carry

    lax.fori_loop(0, Z, fill, 0)

    def edge(s, side, k):
        post = posts[s % 2]
        if side == 0:
            src = post.at[pl.ds(0, 5), :, pl.ds(R - 1, 1), pcols(k)]
            dst = lo.at[s, :, :, pl.ds(R - 1, 1), pcols(k)]
        else:
            src = post.at[pl.ds(5, 5), :, pl.ds(0, 1), pcols(k)]
            dst = hi.at[s, :, :, pl.ds(0, 1), pcols(k)]
        return pltpu.make_async_remote_copy(
            src_ref=src, dst_ref=dst, send_sem=send_sem.at[s, side, k], recv_sem=recv_sem.at[s, side, k],
            device_id=after if side == 0 else before, device_id_type=MESH,
        )

    def poro_edge(side):
        rows = pl.ds(R - 1, 1) if side == 0 else pl.ds(0, 1)
        inner = pl.ds(B, width)
        return pltpu.make_async_remote_copy(
            src_ref=poro.at[:, rows, inner], dst_ref=(plo if side == 0 else phi).at[:, rows, :],
            send_sem=psend.at[side], recv_sem=precv.at[side],
            device_id=after if side == 0 else before, device_id_type=MESH,
        )

    def conc_edge(p, side, k):
        rows = pl.ds(R - 2, 2) if side == 0 else pl.ds(0, 2)
        return pltpu.make_async_remote_copy(
            src_ref=concs[p].at[:, rows, pcols(k)], dst_ref=(clo if side == 0 else chi).at[p, :, rows, cols(k)],
            send_sem=csend.at[p, side, k], recv_sem=crecv.at[p, side, k],
            device_id=after if side == 0 else before, device_id_type=MESH,
        )

    def vel_edge(side, k):
        rows = pl.ds(R - 1, 1) if side == 0 else pl.ds(0, 1)
        return pltpu.make_async_remote_copy(
            src_ref=ux.at[:, rows, cols(k)], dst_ref=(ulo if side == 0 else uhi).at[:, rows, cols(k)],
            send_sem=usend.at[side, k], recv_sem=urecv.at[side, k],
            device_id=after if side == 0 else before, device_id_type=MESH,
        )

    def to_tile(a, k):
        src, dst = (napl, napl_out) if a == 0 else (conc2, conc_out)
        rows = pl.ds(pl.multiple_of(n * R, R), R)
        return pltpu.make_async_remote_copy(
            src_ref=src.at[:, :, cols(k)], dst_ref=dst.at[:, rows, :],
            send_sem=asend.at[a, k], recv_sem=arecv.at[a, n], device_id=(w, k), device_id_type=MESH,
        )

    def from_tile(a, k):
        src, dst = (napl, napl_out) if a == 0 else (conc2, conc_out)
        rows = pl.ds(pl.multiple_of(k * R, R), R)
        return pltpu.make_async_remote_copy(
            src_ref=src.at[:, :, cols(k)], dst_ref=dst.at[:, rows, :],
            send_sem=asend.at[a, k], recv_sem=arecv.at[a, k], device_id=(w, k), device_id_type=MESH,
        )

    def own_tile(a):
        src, dst = (napl, napl_out) if a == 0 else (conc2, conc_out)
        rows = pl.ds(pl.multiple_of(n * R, R), R)
        return pltpu.make_async_copy(src.at[:, :, cols(n)], dst.at[:, rows, :], own_sem.at[a])

    def send_tile(a, k):
        @pl.when(k != n)
        def _():
            to_tile(a, k).start()

        @pl.when(k == n)
        def _():
            own_tile(a).start()

    def blocks(k, fn, carry=0):
        return lax.fori_loop(0, per_chunk, lambda i, c: fn(k * per_chunk + i, c), carry)

    def at(b):
        return pl.ds(pl.multiple_of(b * B, B), B)

    def start_block(b, carry):
        here, there = at(b), at(b + 1)
        for z in range(Z):
            f = [fbuf[q, z, :, here] for q in range(19)]
            out = collide(f, phase[z, :, here])
            for q in range(19):
                post0[SLOT[q], z, :, there] = out[q]
        return carry

    smalls[0].wait()
    load(0).wait()
    blocks(0, start_block)
    pl.semaphore_wait(barrier, narrow + 1)
    for side in range(2):
        edge(0, side, 0).start()
    for copy in smalls[1:3]:
        copy.wait()
    for side in range(2):
        poro_edge(side).start()

    def first_chunk(k, carry):
        load(k).wait()
        blocks(k, start_block)
        for side in range(2):
            edge(0, side, k).start()
        return carry

    lax.fori_loop(1, chunks, first_chunk, 0)
    for side in range(2):
        for k in range(chunks):
            conc_edge(0, side, k).start()
    for copy in smalls[3:]:
        copy.wait()

    def stream(post, s, z, b):
        base = b * B + B

        def block(slot, layer, shift, ex):
            where = pl.ds(pl.multiple_of(base + shift, B), B)
            value = post[slot, layer, :, where]
            if ex == 1:
                value = jnp.where(row == R - 1, lo[s, slot, layer, :, where], value)
            elif ex == -1:
                value = jnp.where(row == 0, hi[s, slot - 5, layer, :, where], value)
            return value

        here = pl.ds(pl.multiple_of(base, B), B)
        f = []
        for q in range(19):
            ex, ey, ez = DIRS[q]
            slot, layer = SLOT[q], (z - ez) % Z
            if q == 0:
                f.append(post[slot, z, :, here])
                continue
            moved = block(slot, layer, 0, ex)
            if ey == 1:
                moved = pltpu.roll(jnp.where(lane == B - 1, block(slot, layer, -B, ex), moved), 1, 1)
            elif ey == -1:
                moved = pltpu.roll(jnp.where(lane == 0, block(slot, layer, B, ex), moved), B - 1, 1)
            if ex:
                moved = pltpu.roll(moved, 1 if ex == 1 else R - 1, 0)
            f.append(jnp.where(moved < jnp.inf, moved, post[SLOT[OPP[q]], z, :, here]))
        return f

    def await_edges(s, k):
        @pl.when(k == 0)
        def _():
            for side in range(2):
                edge(s, side, k).wait_recv()

        @pl.when(k < chunks - 1)
        def _():
            for side in range(2):
                edge(s, side, k + 1).wait_recv()

    def one_step(s):
        old, new = posts[(s + 1) % 2], posts[s % 2]

        def move_block(b, c):
            for z in range(Z):
                out = collide(stream(old, s - 1, z, b), phase[z, :, at(b)])
                for q in range(19):
                    new[SLOT[q], z, :, at(b + 1)] = out[q]
            return c

        def chunk(k, c):
            await_edges(s - 1, k)

            if s >= 2:
                for side in range(2):
                    edge(s - 2, side, k).wait_send()

            blocks(k, move_block)
            for side in range(2):
                edge(s, side, k).start()
            return c

        lax.fori_loop(0, chunks, chunk, 0)

        if s == 1:
            for side in range(2):
                poro_edge(side).wait_recv()

            def coef(b, c):
                here, there, beyond = at(b), at(b + 1), at(b + 2)
                for z in range(Z):
                    own = poro[z, :, there]
                    high = jnp.where(last, flags[1, z : z + 1, here].astype(jnp.float32), phi[z, :, here])
                    low = jnp.where(first, flags[0, z : z + 1, here].astype(jnp.float32), plo[z, :, here])
                    wx[z, :, here] = own * pltpu.roll(jnp.where(row == 0, high, own), R - 1, 0)
                    wl[z, :, here] = low * pltpu.roll(own, R - 1, 0)
                    wy[z, :, here] = own * pltpu.roll(jnp.where(lane == 0, poro[z, :, beyond], own), B - 1, 1)
                    wz[z, :, here] = own * poro[(z + 1) % Z, :, there]
                    inv[z, :, here] = 1.0 / jnp.maximum(own, 0.3)
                return c

            lax.fori_loop(0, width // B, coef, 0)

    for s in range(1, STEPS):
        one_step(s)

    def last_block(b, carry):
        here, there = at(b), at(b + 1)
        for z in range(Z):
            f = stream(posts[(STEPS - 1) % 2], STEPS - 1, z, b)
            solid = phase[z, :, here] == 2
            rho, jx, jy, jz = moments(f)
            per = jnp.where(solid, 0.0, 1.0) / jnp.where(solid, 1.0, rho)
            ux[z, :, here] = jnp.where(solid, 0.0, jx * per)
            uy[z, :, there] = jnp.where(solid, 0.0, jy * per)
            uz[z, :, here] = jnp.where(solid, 0.0, jz * per)
            for q in range(19):
                fbuf[q, z, :, here] = jnp.where(solid, fbuf[q, z, :, here], f[q])
        return carry

    def store(k):
        return pltpu.make_async_copy(
            fbuf.at[:, :, :, cols(k)], pop_out.at[:, :, :, cols(k)], out_sem.at[k]
        )

    def last_chunk(k, carry):
        await_edges(STEPS - 1, k)
        blocks(k, last_block)
        for side in range(2):
            vel_edge(side, k).start()
        store(k).start()
        return carry

    lax.fori_loop(0, chunks, last_chunk, 0)

    def transport(step, b, carry):
        here, there, back, beyond = at(b), at(b + 1), at(b), at(b + 2)
        conc = concs[step]
        c = [conc[z, :, there] for z in range(Z)]
        if step == 0:
            for z in range(Z):
                vx = ux[z, :, here]
                high = jnp.where(last, pltpu.roll(vx, 1, 0), uhi[z, :, here])
                low = jnp.where(first, pltpu.roll(vx, R - 1, 0), ulo[z, :, here])
                nxt = pltpu.roll(vx, R - 1, 0)
                ax[z, :, here] = wx[z, :, here] * (0.5 * (vx + jnp.where(row == R - 1, pltpu.roll(high, R - 1, 0), nxt)))
                al[z, :, here] = wl[z, :, here] * (0.5 * (low + nxt))
                vy = uy[z, :, there]
                ay[z, :, here] = wy[z, :, here] * (
                    0.5 * (vy + pltpu.roll(jnp.where(lane == 0, uy[z, :, beyond], vy), B - 1, 1))
                )
                az[z, :, here] = wz[z, :, here] * (0.5 * (uz[z, :, here] + uz[(z + 1) % Z, :, here]))
        zflux = [
            face_flux(
                c[(z - 1) % Z], c[z], c[(z + 1) % Z], c[(z + 2) % Z], wz[z, :, here], az[z, :, here]
            )
            for z in range(Z)
        ]
        flow = []
        for z in range(Z):
            own = c[z]
            high = chi[step, z, :, here]
            low = clo[step, z, :, here]
            up1, up2 = pltpu.roll(own, R - 1, 0), pltpu.roll(own, R - 2, 0)
            low = jnp.where(first, 0.0, low)
            down1 = pltpu.roll(jnp.where(row == R - 1, low, own), 1, 0)
            end = pltpu.roll(own, 1, 0)
            one = jnp.where(last, end, high)
            two = jnp.where(last, jnp.where(row == 0, end, pltpu.roll(own, 2, 0)), high)
            ahead = pltpu.roll(jnp.where(row == 0, one, own), R - 1, 0)
            far = pltpu.roll(jnp.where(row < 2, two, own), R - 2, 0)
            xflux = face_flux(down1, own, ahead, far, wx[z, :, here], ax[z, :, here])
            xlow = face_flux(pltpu.roll(low, 1, 0), low, up1, up2, wl[z, :, here], al[z, :, here])
            change = pltpu.roll(jnp.where(row == R - 1, xlow, xflux), 1, 0) - xflux
            cb, cn = conc[z, :, back], conc[z, :, beyond]
            left = pltpu.roll(jnp.where(lane == B - 1, cb, own), 1, 1)
            right = pltpu.roll(jnp.where(lane == 0, cn, own), B - 1, 1)
            right2 = pltpu.roll(jnp.where(lane < 2, cn, own), B - 2, 1)
            yflux = face_flux(left, own, right, right2, wy[z, :, here], ay[z, :, here])
            flow.append(yflux)
            change = change + (pltpu.roll(jnp.where(lane == B - 1, carry[z], yflux), 1, 1) - yflux)
            change = change + (zflux[(z - 1) % Z] - zflux[z])
            s = napl[z, :, here]
            if step == 0:
                rate = 0.3 * s * (1.0 - own)
                new = own + (change + rate) * inv[z, :, here]
                conc1[z, :, there] = new
                s = s - 0.5 * rate
                rate = 0.3 * s * (1.0 - new)
                napl[z, :, here] = s - 0.5 * rate
                rate_buf[z, :, here] = rate
            else:
                conc2[z, :, here] = own + (change + rate_buf[z, :, here]) * inv[z, :, here]
        return tuple(flow)

    def first_transport(k, carry):
        for side in range(2):
            vel_edge(side, k).wait_recv()
            conc_edge(0, side, k).wait_recv()
        carry = blocks(k, functools.partial(transport, 0), carry)
        for side in range(2):
            conc_edge(1, side, k).start()
        send_tile(0, k)
        return carry

    def second_transport(k, carry):
        for side in range(2):
            conc_edge(1, side, k).wait_recv()
        carry = blocks(k, functools.partial(transport, 1), carry)
        send_tile(1, k)
        return carry

    still = (zero,) * Z
    lax.fori_loop(0, chunks, first_transport, still)
    lax.fori_loop(0, chunks, second_transport, still)

    def settle(k, carry):
        for side in range(2):
            for s in (STEPS - 2, STEPS - 1):
                edge(s, side, k).wait_send()
            vel_edge(side, k).wait_send()
            for p in range(2):
                conc_edge(p, side, k).wait_send()
        store(k).wait()
        return carry

    lax.fori_loop(0, chunks, settle, 0)
    for side in range(2):
        poro_edge(side).wait_send()

    def settle_tile(k, carry):
        @pl.when(k != n)
        def _():
            for a in range(2):
                to_tile(a, k).wait_send()
                from_tile(a, k).wait_recv()

        return carry

    lax.fori_loop(0, chunks, settle_tile, 0)
    for a in range(2):
        own_tile(a).wait()


def local(wide, narrow, populations, phase, porosity, napl, concentration, flags):
    width = phase.shape[2]
    tile = width // narrow
    padded = width + 2 * B
    f32 = jnp.float32
    DMA = pltpu.SemaphoreType.DMA

    def full():
        return pltpu.VMEM((Z, R, width), f32)

    any_space = pl.BlockSpec(memory_space=pl.ANY)
    scratch = [
        pltpu.VMEM((19, Z, R, width), f32),
        pltpu.VMEM((Z, R, width), jnp.int32),
        pltpu.VMEM((Z, R, padded), f32),
        full(),
        pltpu.VMEM((Z, R, padded), f32), pltpu.VMEM((Z, R, padded), f32),
        full(), full(),
        pltpu.VMEM((2, Z, width), jnp.int32),
        pltpu.VMEM((19, Z, R, padded), f32), pltpu.VMEM((19, Z, R, padded), f32),
        pltpu.VMEM((STEPS, 5, Z, R, padded), f32),
        pltpu.VMEM((STEPS, 5, Z, R, padded), f32),
        full(), full(),
        pltpu.VMEM((2, Z, R, width), f32), pltpu.VMEM((2, Z, R, width), f32),
        full(), full(),
        full(), pltpu.VMEM((Z, R, padded), f32), full(),
        full(), full(), full(), full(),
        full(), full(), full(), full(),
        full(),
        DMA((narrow,)), DMA((5,)), DMA((narrow,)), DMA((2,)),
        DMA((STEPS, 2, narrow)), DMA((STEPS, 2, narrow)),
        DMA((2,)), DMA((2,)),
        DMA((2, 2, narrow)), DMA((2, 2, narrow)),
        DMA((2, narrow)), DMA((2, narrow)),
        DMA((2, narrow)), DMA((2, narrow)),
    ]
    tiles = jax.ShapeDtypeStruct((Z, R * narrow, tile), f32)
    return pl.pallas_call(
        functools.partial(body, wide, narrow, width, tile),
        out_shape=(jax.ShapeDtypeStruct(populations.shape, f32), tiles, tiles),
        in_specs=[any_space] * 6,
        out_specs=(any_space,) * 3,
        scratch_shapes=scratch,
        compiler_params=pltpu.CompilerParams(
            collective_id=0, has_side_effects=True, vmem_limit_bytes=56 * 2**20
        ),
        name="dissolution",
    )(populations, phase, porosity, napl, concentration, flags)


def solution(mesh):
    strips = ("wide", "narrow")
    in_specs = (
        P(None, None, strips, None),
        P(None, strips, None),
        P(None, strips, None),
        P(None, strips, None),
        P(None, strips, None),
        P(),
    )
    out_specs = (
        P(None, None, strips, None),
        P(None, "wide", "narrow"),
        P(None, "wide", "narrow"),
    )
    fn = functools.partial(local, mesh.shape["wide"], mesh.shape["narrow"])
    return jax.shard_map(fn, mesh=mesh, in_specs=in_specs, out_specs=out_specs, check_vma=False)
```

```python
import functools

import jax
import jax.numpy as jnp
from jax import lax
from jax.experimental import pallas as pl
from jax.experimental.pallas import tpu as pltpu
from jax.sharding import PartitionSpec as P

MESH = pl.DeviceIdType.MESH
DIRS = [
    (0, 0, 0), (1, 0, 0), (-1, 0, 0), (0, 1, 0), (0, -1, 0), (0, 0, 1), (0, 0, -1),
    (1, 1, 0), (-1, -1, 0), (1, -1, 0), (-1, 1, 0), (1, 0, 1), (-1, 0, -1), (1, 0, -1), (-1, 0, 1),
    (0, 1, 1), (0, -1, -1), (0, 1, -1), (0, -1, 1),
]
OPP = [0, 2, 1, 4, 3, 6, 5, 8, 7, 10, 9, 12, 11, 14, 13, 16, 15, 18, 17]
UP = [1, 7, 9, 11, 13]
DOWN = [2, 8, 10, 12, 14]
ORDER = UP + DOWN + [0, 3, 4, 5, 6, 15, 16, 17, 18]
SLOT = {q: i for i, q in enumerate(ORDER)}
STEPS = 4
PARTS = 8
Z = 4
R = 8
B = 128


def collide(f, phase):
    total, diff = {}, {}
    for q in range(1, 19, 2):
        total[q] = f[q] + f[q + 1]
        diff[q] = f[q] - f[q + 1]
    rho = (
        ((f[0] + total[1]) + (total[3] + total[5]))
        + ((total[7] + total[9]) + (total[11] + total[13]))
        + (total[15] + total[17])
    )
    jx = (diff[1] + diff[7]) + (diff[9] + diff[11]) + diff[13]
    jy = (diff[3] + diff[7]) + (diff[15] - diff[9]) + diff[17]
    jz = (diff[5] + diff[11]) + (diff[15] - diff[13]) - diff[17]
    rho = jnp.where(phase == 2, jnp.nan, rho)
    factor = jnp.where(phase == 1, 0.5, 1.0)
    per = factor / rho
    vx, vy, vz = jx * per, jy * per, jz * per
    factor = factor * (3.75 / 36.0)
    nx, ny, nz = jx * factor, jy * factor, jz * factor
    hx, hy, hz = vx * 1.5, vy * 1.5, vz * 1.5
    sxx, syy, szz = nx * hx, ny * hy, nz * hz
    hx, hy = hx + hx, hy + hy
    xy, xz, yz = ny * hx, nz * hx, nz * hy
    even = rho * (1.25 / 36.0) - (sxx + syy + szz) * (1.0 / 3.0)
    post = [None] * 19
    post[0] = 12.0 * even - 0.25 * f[0]

    def pair(q, e, o):
        post[q] = (e + o) - 0.25 * f[q]
        post[q + 1] = (e - o) - 0.25 * f[q + 1]

    ex, ey, ez = even + sxx, even + syy, even + szz
    pair(1, ex + ex, nx + nx)
    pair(3, ey + ey, ny + ny)
    pair(5, ez + ez, nz + nz)
    exy, exz, eyz = ex + syy, ex + szz, ey + szz
    pair(7, exy + xy, nx + ny)
    pair(9, exy - xy, nx - ny)
    pair(11, exz + xz, nx + nz)
    pair(13, exz - xz, nx - nz)
    pair(15, eyz + yz, ny + nz)
    pair(17, eyz - yz, ny - nz)
    return post


def moments(f):
    total, diff = {}, {}
    for q in range(1, 19, 2):
        total[q] = f[q] + f[q + 1]
        diff[q] = f[q] - f[q + 1]
    rho = (
        ((f[0] + total[1]) + (total[3] + total[5]))
        + ((total[7] + total[9]) + (total[11] + total[13]))
        + (total[15] + total[17])
    )
    jx = (diff[1] + diff[7]) + (diff[9] + diff[11]) + diff[13]
    jy = (diff[3] + diff[7]) + (diff[15] - diff[9]) + diff[17]
    jz = (diff[5] + diff[11]) + (diff[15] - diff[13]) - diff[17]
    return rho, jx, jy, jz


def half_minmod(p, q):
    return 0.5 * jnp.maximum(jnp.minimum(p, q), jnp.minimum(jnp.maximum(p, q), 0.0))


def face_flux(back, here, ahead, far, w, a):
    step = ahead - here
    up = here + half_minmod(here - back, step)
    down = ahead - half_minmod(step, far - ahead)
    return a * jnp.where(a > 0, up, down) - (0.15 * w) * step


def body(
    wide, narrow, width, tile,
    pop_in, phase_in, poro_in, napl_in, conc_in, flags_in,
    pop_out, conc_out, napl_out,
    fbuf, phase, poro, napl, conc0, conc1, conc2, napl2, rate_buf, inner, flags, post0, post1, lo, hi,
    plo, phi, clo, chi, ulo, uhi, ux, uy, uz, wx, wl, wy, wz, ax, al, ay, az, inv,
    load_sem, small_sem, own_sem,
    send_sem, recv_sem, psend, precv, csend, crecv, usend, urecv, asend, arecv,
):
    posts, concs = (post0, post1), (conc0, conc1)
    w, n = lax.axis_index("wide"), lax.axis_index("narrow")
    chunks = narrow
    per_chunk = tile // B
    parts = PARTS
    part = width // parts
    strip = w * narrow + n

    def neighbour(offset):
        g = lax.rem(strip + offset + wide * narrow, wide * narrow)
        return (g // narrow, lax.rem(g, narrow))

    after, before = neighbour(1), neighbour(-1)
    first, last = strip == 0, strip == wide * narrow - 1

    def part_cols(k):
        return pl.ds(pl.multiple_of(B + k * part, B), part)

    def cols(k):
        return pl.ds(pl.multiple_of(k * tile, tile), tile)

    def pcols(k):
        return pl.ds(pl.multiple_of(B + k * tile, B), tile)

    def load(k):
        return pltpu.make_async_copy(
            pop_in.at[:, :, :, cols(k)], fbuf.at[:, :, :, cols(k)], load_sem.at[k]
        )

    smalls = [
        pltpu.make_async_copy(phase_in, phase, small_sem.at[0]),
        pltpu.make_async_copy(poro_in, poro.at[:, :, pl.ds(B, width)], small_sem.at[1]),
        pltpu.make_async_copy(conc_in, conc0.at[:, :, pl.ds(B, width)], small_sem.at[2]),
        pltpu.make_async_copy(napl_in, napl, small_sem.at[3]),
        pltpu.make_async_copy(flags_in, flags, small_sem.at[4]),
    ]
    smalls[0].start()
    load(0).start()
    for copy in smalls[1:]:
        copy.start()
    for k in range(1, chunks):
        load(k).start()

    barrier = pltpu.get_barrier_semaphore()
    pl.semaphore_signal(barrier, inc=1, device_id=after, device_id_type=MESH)
    pl.semaphore_signal(barrier, inc=1, device_id=before, device_id_type=MESH)
    for k in range(1, narrow):
        pl.semaphore_signal(
            barrier, inc=1, device_id=(w, lax.rem(n + k, narrow)), device_id_type=MESH
        )

    lane = lax.broadcasted_iota(jnp.int32, (R, B), 1)
    row = lax.broadcasted_iota(jnp.int32, (R, B), 0)
    nan = jnp.full((R, B), jnp.nan, jnp.float32)
    zero = jnp.zeros((R, B), jnp.float32)
    ends = (pl.ds(0, B), pl.ds(B + width, B))

    def fill(z, carry):
        for end in ends:
            for p in range(2):
                for q in range(19):
                    if DIRS[q][1]:
                        posts[p][SLOT[q], z, :, end] = nan
            for s in range(STEPS):
                for m in (1, 2):
                    lo[s, m, z, :, end] = nan
                    hi[s, m, z, :, end] = nan
            poro[z, :, end] = zero
            uy[z, :, end] = zero
            for p in range(2):
                concs[p][z, :, end] = zero
        return carry

    lax.fori_loop(0, Z, fill, 0)

    def edge(s, side, k):
        post = posts[s % 2]
        if side == 0:
            src = post.at[pl.ds(0, 5), :, pl.ds(R - 1, 1), part_cols(k)]
            dst = lo.at[s, :, :, pl.ds(R - 1, 1), part_cols(k)]
        else:
            src = post.at[pl.ds(5, 5), :, pl.ds(0, 1), part_cols(k)]
            dst = hi.at[s, :, :, pl.ds(0, 1), part_cols(k)]
        return pltpu.make_async_remote_copy(
            src_ref=src, dst_ref=dst, send_sem=send_sem.at[s, side, k], recv_sem=recv_sem.at[s, side, k],
            device_id=after if side == 0 else before, device_id_type=MESH,
        )

    def poro_edge(side):
        rows = pl.ds(R - 1, 1) if side == 0 else pl.ds(0, 1)
        inner = pl.ds(B, width)
        return pltpu.make_async_remote_copy(
            src_ref=poro.at[:, rows, inner], dst_ref=(plo if side == 0 else phi).at[:, rows, :],
            send_sem=psend.at[side], recv_sem=precv.at[side],
            device_id=after if side == 0 else before, device_id_type=MESH,
        )

    def conc_edge(p, side, k):
        rows = pl.ds(R - 2, 2) if side == 0 else pl.ds(0, 2)
        src, dst = (pl.ds(B, width), pl.ds(0, width)) if p == 0 else (pcols(k), cols(k))
        return pltpu.make_async_remote_copy(
            src_ref=concs[p].at[:, rows, src], dst_ref=(clo if side == 0 else chi).at[p, :, rows, dst],
            send_sem=csend.at[p, side, k], recv_sem=crecv.at[p, side, k],
            device_id=after if side == 0 else before, device_id_type=MESH,
        )

    def vel_edge(side, k):
        rows = pl.ds(R - 1, 1) if side == 0 else pl.ds(0, 1)
        return pltpu.make_async_remote_copy(
            src_ref=ux.at[:, rows, cols(k)], dst_ref=(ulo if side == 0 else uhi).at[:, rows, cols(k)],
            send_sem=usend.at[side, k], recv_sem=urecv.at[side, k],
            device_id=after if side == 0 else before, device_id_type=MESH,
        )

    def to_tile(a, k):
        src, dst = (napl2, napl_out) if a == 0 else (conc2, conc_out)
        rows = pl.ds(pl.multiple_of(n * R, R), R)
        return pltpu.make_async_remote_copy(
            src_ref=src.at[:, :, cols(k)], dst_ref=dst.at[:, rows, :],
            send_sem=asend.at[a, k], recv_sem=arecv.at[a, n], device_id=(w, k), device_id_type=MESH,
        )

    def from_tile(a, k):
        src, dst = (napl2, napl_out) if a == 0 else (conc2, conc_out)
        rows = pl.ds(pl.multiple_of(k * R, R), R)
        return pltpu.make_async_remote_copy(
            src_ref=src.at[:, :, cols(k)], dst_ref=dst.at[:, rows, :],
            send_sem=asend.at[a, k], recv_sem=arecv.at[a, k], device_id=(w, k), device_id_type=MESH,
        )

    def own_tile(a):
        src, dst = (napl2, napl_out) if a == 0 else (conc2, conc_out)
        rows = pl.ds(pl.multiple_of(n * R, R), R)
        return pltpu.make_async_copy(src.at[:, :, cols(n)], dst.at[:, rows, :], own_sem.at[a])

    def send_tile(a, k):
        @pl.when(k != n)
        def _():
            to_tile(a, k).start()

        @pl.when(k == n)
        def _():
            own_tile(a).start()

    def blocks(k, fn, carry=0, count=per_chunk):
        return lax.fori_loop(0, count, lambda i, c: fn(k * count + i, c), carry)

    def at(b):
        return pl.ds(pl.multiple_of(b * B, B), B)

    def start_block(b, carry):
        here, there = at(b), at(b + 1)
        for z in range(Z):
            f = [fbuf[q, z, :, here] for q in range(19)]
            out = collide(f, phase[z, :, here])
            for q in range(19):
                post0[SLOT[q], z, :, there] = out[q]
        return carry

    per_part, ratio = part // B, parts // chunks
    smalls[0].wait()
    load(0).wait()
    blocks(0, start_block, 0, per_part)
    pl.semaphore_wait(barrier, narrow + 1)
    for side in range(2):
        edge(0, side, 0).start()

    def first_part(k, carry):
        @pl.when(lax.rem(k, ratio) == 0)
        def _():
            load(k // ratio).wait()

        blocks(k, start_block, 0, per_part)
        for side in range(2):
            edge(0, side, k).start()
        return carry

    lax.fori_loop(1, parts, first_part, 0)
    for copy in smalls[1:]:
        copy.wait()
    for side in range(2):
        poro_edge(side).start()

    def stream(post, s, z, b):
        base = b * B + B

        def block(slot, layer, shift, ex):
            where = pl.ds(pl.multiple_of(base + shift, B), B)
            value = post[slot, layer, :, where]
            if ex == 1:
                value = jnp.where(row == R - 1, lo[s, slot, layer, :, where], value)
            elif ex == -1:
                value = jnp.where(row == 0, hi[s, slot - 5, layer, :, where], value)
            return value

        here = pl.ds(pl.multiple_of(base, B), B)
        f = []
        for q in range(19):
            ex, ey, ez = DIRS[q]
            slot, layer = SLOT[q], (z - ez) % Z
            if q == 0:
                f.append(post[slot, z, :, here])
                continue
            moved = block(slot, layer, 0, ex)
            if ey == 1:
                moved = pltpu.roll(jnp.where(lane == B - 1, block(slot, layer, -B, ex), moved), 1, 1)
            elif ey == -1:
                moved = pltpu.roll(jnp.where(lane == 0, block(slot, layer, B, ex), moved), B - 1, 1)
            if ex:
                moved = pltpu.roll(moved, 1 if ex == 1 else R - 1, 0)
            f.append(jnp.where(moved < jnp.inf, moved, post[SLOT[OPP[q]], z, :, here]))
        return f

    def await_edges(s, k):
        @pl.when(k == 0)
        def _():
            for side in range(2):
                edge(s, side, k).wait_recv()

        @pl.when(k < parts - 1)
        def _():
            for side in range(2):
                edge(s, side, k + 1).wait_recv()

    def one_step(s):
        old, new = posts[(s + 1) % 2], posts[s % 2]

        def move_block(b, c):
            for z in range(Z):
                out = collide(stream(old, s - 1, z, b), phase[z, :, at(b)])
                for q in range(19):
                    new[SLOT[q], z, :, at(b + 1)] = out[q]
            return c

        def chunk(k, c):
            await_edges(s - 1, k)

            if s >= 2:
                for side in range(2):
                    edge(s - 2, side, k).wait_send()

            blocks(k, move_block, 0, per_part)
            for side in range(2):
                edge(s, side, k).start()
            return c

        lax.fori_loop(0, parts, chunk, 0)

        if s == 1:
            for side in range(2):
                conc_edge(0, side, 0).start()
        if s == 2:
            for side in range(2):
                poro_edge(side).wait_recv()

            def coef(b, c):
                here, there, beyond = at(b), at(b + 1), at(b + 2)
                for z in range(Z):
                    own = poro[z, :, there]
                    high = jnp.where(last, flags[1, z : z + 1, here].astype(jnp.float32), phi[z, :, here])
                    low = jnp.where(first, flags[0, z : z + 1, here].astype(jnp.float32), plo[z, :, here])
                    wx[z, :, here] = own * pltpu.roll(jnp.where(row == 0, high, own), R - 1, 0)
                    wl[z, :, here] = low * pltpu.roll(own, R - 1, 0)
                    wy[z, :, here] = own * pltpu.roll(jnp.where(lane == 0, poro[z, :, beyond], own), B - 1, 1)
                    wz[z, :, here] = own * poro[(z + 1) % Z, :, there]
                    inv[z, :, here] = 1.0 / jnp.maximum(own, 0.3)
                return c

            lax.fori_loop(0, width // B, coef, 0)

    for s in range(1, STEPS):
        one_step(s)

    def last_block(b, carry):
        here, there = at(b), at(b + 1)
        for z in range(Z):
            f = stream(posts[(STEPS - 1) % 2], STEPS - 1, z, b)
            solid = phase[z, :, here] == 2
            rho, jx, jy, jz = moments(f)
            per = jnp.where(solid, 0.0, 1.0) / jnp.where(solid, 1.0, rho)
            ux[z, :, here] = jnp.where(solid, 0.0, jx * per)
            uy[z, :, there] = jnp.where(solid, 0.0, jy * per)
            uz[z, :, here] = jnp.where(solid, 0.0, jz * per)
            for q in range(19):
                pop_out[q, z, :, here] = jnp.where(solid, fbuf[q, z, :, here], f[q])
        return carry

    def last_part(k, carry):
        await_edges(STEPS - 1, k)
        blocks(k, last_block, 0, per_part)

        @pl.when(lax.rem(k, ratio) == ratio - 1)
        def _():
            for side in range(2):
                vel_edge(side, k // ratio).start()

        return carry

    lax.fori_loop(0, parts, last_part, 0)

    def inner_flux(step, b, carry):
        here, there, back, beyond = at(b), at(b + 1), at(b), at(b + 2)
        conc = concs[step]
        c = [conc[z, :, there] for z in range(Z)]
        if step == 0:
            for z in range(Z):
                vy = uy[z, :, there]
                ay[z, :, here] = wy[z, :, here] * (
                    0.5 * (vy + pltpu.roll(jnp.where(lane == 0, uy[z, :, beyond], vy), B - 1, 1))
                )
                az[z, :, here] = wz[z, :, here] * (0.5 * (uz[z, :, here] + uz[(z + 1) % Z, :, here]))
        zflux = [
            face_flux(
                c[(z - 1) % Z], c[z], c[(z + 1) % Z], c[(z + 2) % Z], wz[z, :, here], az[z, :, here]
            )
            for z in range(Z)
        ]
        flow = []
        for z in range(Z):
            own = c[z]
            cb, cn = conc[z, :, back], conc[z, :, beyond]
            left = pltpu.roll(jnp.where(lane == B - 1, cb, own), 1, 1)
            right = pltpu.roll(jnp.where(lane == 0, cn, own), B - 1, 1)
            right2 = pltpu.roll(jnp.where(lane < 2, cn, own), B - 2, 1)
            yflux = face_flux(left, own, right, right2, wy[z, :, here], ay[z, :, here])
            flow.append(yflux)
            change = pltpu.roll(jnp.where(lane == B - 1, carry[z], yflux), 1, 1) - yflux
            inner[z, :, here] = change + (zflux[(z - 1) % Z] - zflux[z])
        return tuple(flow)

    def transport(step, b, carry):
        here, there = at(b), at(b + 1)
        conc = concs[step]
        for z in range(Z):
            own = conc[z, :, there]
            high = chi[step, z, :, here]
            low = jnp.where(first, 0.0, clo[step, z, :, here])
            if step == 0:
                vx = ux[z, :, here]
                vhigh = jnp.where(last, pltpu.roll(vx, 1, 0), uhi[z, :, here])
                vlow = jnp.where(first, pltpu.roll(vx, R - 1, 0), ulo[z, :, here])
                nxt = pltpu.roll(vx, R - 1, 0)
                a = wx[z, :, here] * (0.5 * (vx + jnp.where(row == R - 1, pltpu.roll(vhigh, R - 1, 0), nxt)))
                e = wl[z, :, here] * (0.5 * (vlow + nxt))
                ax[z, :, here] = a
                al[z, :, here] = e
            else:
                a, e = ax[z, :, here], al[z, :, here]
            up1, up2 = pltpu.roll(own, R - 1, 0), pltpu.roll(own, R - 2, 0)
            down1 = pltpu.roll(jnp.where(row == R - 1, low, own), 1, 0)
            end = pltpu.roll(own, 1, 0)
            one = jnp.where(last, end, high)
            two = jnp.where(last, jnp.where(row == 0, end, pltpu.roll(own, 2, 0)), high)
            ahead = pltpu.roll(jnp.where(row == 0, one, own), R - 1, 0)
            far = pltpu.roll(jnp.where(row < 2, two, own), R - 2, 0)
            xflux = face_flux(down1, own, ahead, far, wx[z, :, here], a)
            xlow = face_flux(pltpu.roll(low, 1, 0), low, up1, up2, wl[z, :, here], e)
            change = pltpu.roll(jnp.where(row == R - 1, xlow, xflux), 1, 0) - xflux
            change = change + inner[z, :, here]
            if step == 0:
                s = napl[z, :, here]
                rate = 0.3 * s * (1.0 - own)
                new = own + (change + rate) * inv[z, :, here]
                conc1[z, :, there] = new
                s = s - 0.5 * rate
                rate = 0.3 * s * (1.0 - new)
                napl2[z, :, here] = s - 0.5 * rate
                rate_buf[z, :, here] = rate
            else:
                conc2[z, :, here] = own + (change + rate_buf[z, :, here]) * inv[z, :, here]
        return carry

    def first_transport(k, carry):
        for side in range(2):
            vel_edge(side, k).wait_recv()
        blocks(k, functools.partial(transport, 0))
        for side in range(2):
            conc_edge(1, side, k).start()
        send_tile(0, k)
        return carry

    def second_transport(k, carry):
        for side in range(2):
            conc_edge(1, side, k).wait_recv()
        blocks(k, functools.partial(transport, 1))
        send_tile(1, k)
        return carry

    still = (zero,) * Z
    lax.fori_loop(0, width // B, functools.partial(inner_flux, 0), still)
    for side in range(2):
        conc_edge(0, side, 0).wait_recv()
    lax.fori_loop(0, chunks, first_transport, 0)
    lax.fori_loop(0, width // B, functools.partial(inner_flux, 1), still)
    lax.fori_loop(0, chunks, second_transport, 0)

    def settle_part(k, carry):
        for side in range(2):
            for s in (STEPS - 2, STEPS - 1):
                edge(s, side, k).wait_send()
        return carry

    def settle(k, carry):
        for side in range(2):
            vel_edge(side, k).wait_send()
            conc_edge(1, side, k).wait_send()
        return carry

    lax.fori_loop(0, parts, settle_part, 0)
    lax.fori_loop(0, chunks, settle, 0)
    for side in range(2):
        poro_edge(side).wait_send()
        conc_edge(0, side, 0).wait_send()

    def settle_tile(k, carry):
        @pl.when(k != n)
        def _():
            for a in range(2):
                to_tile(a, k).wait_send()
                from_tile(a, k).wait_recv()

        return carry

    lax.fori_loop(0, chunks, settle_tile, 0)
    for a in range(2):
        own_tile(a).wait()


def local(wide, narrow, populations, phase, porosity, napl, concentration, flags):
    width = phase.shape[2]
    tile = width // narrow
    padded = width + 2 * B
    f32 = jnp.float32
    DMA = pltpu.SemaphoreType.DMA

    def full():
        return pltpu.VMEM((Z, R, width), f32)

    any_space = pl.BlockSpec(memory_space=pl.ANY)
    scratch = [
        pltpu.VMEM((19, Z, R, width), f32),
        pltpu.VMEM((Z, R, width), jnp.int32),
        pltpu.VMEM((Z, R, padded), f32),
        full(),
        pltpu.VMEM((Z, R, padded), f32), pltpu.VMEM((Z, R, padded), f32),
        full(), full(), full(), full(),
        pltpu.VMEM((2, Z, width), jnp.int32),
        pltpu.VMEM((19, Z, R, padded), f32), pltpu.VMEM((19, Z, R, padded), f32),
        pltpu.VMEM((STEPS, 5, Z, R, padded), f32),
        pltpu.VMEM((STEPS, 5, Z, R, padded), f32),
        full(), full(),
        pltpu.VMEM((2, Z, R, width), f32), pltpu.VMEM((2, Z, R, width), f32),
        full(), full(),
        full(), pltpu.VMEM((Z, R, padded), f32), full(),
        full(), full(), full(), full(),
        full(), full(), full(), full(),
        full(),
        DMA((narrow,)), DMA((5,)), DMA((2,)),
        DMA((STEPS, 2, PARTS)), DMA((STEPS, 2, PARTS)),
        DMA((2,)), DMA((2,)),
        DMA((2, 2, narrow)), DMA((2, 2, narrow)),
        DMA((2, narrow)), DMA((2, narrow)),
        DMA((2, narrow)), DMA((2, narrow)),
    ]
    tiles = jax.ShapeDtypeStruct((Z, R * narrow, tile), f32)
    return pl.pallas_call(
        functools.partial(body, wide, narrow, width, tile),
        out_shape=(pltpu.VMEM(populations.shape, f32),) + (pltpu.VMEM(tiles.shape, f32),) * 2,
        in_specs=[any_space] * 6,
        out_specs=(pl.BlockSpec(memory_space=pltpu.VMEM),) * 3,
        scratch_shapes=scratch,
        compiler_params=pltpu.CompilerParams(
            collective_id=0, has_side_effects=True, vmem_limit_bytes=56 * 2**20
        ),
        name="dissolution",
    )(populations, phase, porosity, napl, concentration, flags)


def solution(mesh):
    strips = ("wide", "narrow")
    in_specs = (
        P(None, None, strips, None),
        P(None, strips, None),
        P(None, strips, None),
        P(None, strips, None),
        P(None, strips, None),
        P(),
    )
    out_specs = (
        P(None, None, strips, None),
        P(None, "wide", "narrow"),
        P(None, "wide", "narrow"),
    )
    fn = functools.partial(local, mesh.shape["wide"], mesh.shape["narrow"])
    return jax.shard_map(fn, mesh=mesh, in_specs=in_specs, out_specs=out_specs, check_vma=False)
```

```python
import functools

import jax
import jax.numpy as jnp
from jax import lax
from jax.experimental import pallas as pl
from jax.experimental.pallas import tpu as pltpu
from jax.sharding import PartitionSpec as P

MESH = pl.DeviceIdType.MESH
DIRS = [
    (0, 0, 0), (1, 0, 0), (-1, 0, 0), (0, 1, 0), (0, -1, 0), (0, 0, 1), (0, 0, -1),
    (1, 1, 0), (-1, -1, 0), (1, -1, 0), (-1, 1, 0), (1, 0, 1), (-1, 0, -1), (1, 0, -1), (-1, 0, 1),
    (0, 1, 1), (0, -1, -1), (0, 1, -1), (0, -1, 1),
]
OPP = [0, 2, 1, 4, 3, 6, 5, 8, 7, 10, 9, 12, 11, 14, 13, 16, 15, 18, 17]
UP = [1, 7, 9, 11, 13]
DOWN = [2, 8, 10, 12, 14]
ORDER = UP + DOWN + [0, 3, 4, 5, 6, 15, 16, 17, 18]
SLOT = {q: i for i, q in enumerate(ORDER)}
STEPS = 4
PARTS = 8
Z = 4
R = 8
B = 128


def collide(f, phase):
    total, diff = {}, {}
    for q in range(1, 19, 2):
        total[q] = f[q] + f[q + 1]
        diff[q] = f[q] - f[q + 1]
    rho = (
        ((f[0] + total[1]) + (total[3] + total[5]))
        + ((total[7] + total[9]) + (total[11] + total[13]))
        + (total[15] + total[17])
    )
    jx = (diff[1] + diff[7]) + (diff[9] + diff[11]) + diff[13]
    jy = (diff[3] + diff[7]) + (diff[15] - diff[9]) + diff[17]
    jz = (diff[5] + diff[11]) + (diff[15] - diff[13]) - diff[17]
    rho = jnp.where(phase == 2, jnp.nan, rho)
    factor = jnp.where(phase == 1, 0.5, 1.0)
    per = factor / rho
    vx, vy, vz = jx * per, jy * per, jz * per
    factor = factor * (3.75 / 36.0)
    nx, ny, nz = jx * factor, jy * factor, jz * factor
    hx, hy, hz = vx * 1.5, vy * 1.5, vz * 1.5
    sxx, syy, szz = nx * hx, ny * hy, nz * hz
    hx, hy = hx + hx, hy + hy
    xy, xz, yz = ny * hx, nz * hx, nz * hy
    even = rho * (1.25 / 36.0) - (sxx + syy + szz) * (1.0 / 3.0)
    post = [None] * 19
    post[0] = 12.0 * even - 0.25 * f[0]

    def pair(q, e, o):
        post[q] = (e + o) - 0.25 * f[q]
        post[q + 1] = (e - o) - 0.25 * f[q + 1]

    ex, ey, ez = even + sxx, even + syy, even + szz
    pair(1, ex + ex, nx + nx)
    pair(3, ey + ey, ny + ny)
    pair(5, ez + ez, nz + nz)
    exy, exz, eyz = ex + syy, ex + szz, ey + szz
    pair(7, exy + xy, nx + ny)
    pair(9, exy - xy, nx - ny)
    pair(11, exz + xz, nx + nz)
    pair(13, exz - xz, nx - nz)
    pair(15, eyz + yz, ny + nz)
    pair(17, eyz - yz, ny - nz)
    return post


def moments(f):
    total, diff = {}, {}
    for q in range(1, 19, 2):
        total[q] = f[q] + f[q + 1]
        diff[q] = f[q] - f[q + 1]
    rho = (
        ((f[0] + total[1]) + (total[3] + total[5]))
        + ((total[7] + total[9]) + (total[11] + total[13]))
        + (total[15] + total[17])
    )
    jx = (diff[1] + diff[7]) + (diff[9] + diff[11]) + diff[13]
    jy = (diff[3] + diff[7]) + (diff[15] - diff[9]) + diff[17]
    jz = (diff[5] + diff[11]) + (diff[15] - diff[13]) - diff[17]
    return rho, jx, jy, jz


def half_minmod(p, q):
    return 0.5 * jnp.maximum(jnp.minimum(p, q), jnp.minimum(jnp.maximum(p, q), 0.0))


def face_flux(back, here, ahead, far, w, a):
    step = ahead - here
    up = here + half_minmod(here - back, step)
    down = ahead - half_minmod(step, far - ahead)
    return a * jnp.where(a > 0, up, down) - (0.15 * w) * step


def body(
    wide, narrow, width, tile,
    pop_in, phase_in, poro_in, napl_in, conc_in, flags_in,
    pop_out, conc_out, napl_out,
    fbuf, phase, poro, napl, conc0, conc1, conc2, napl2, rate_buf, inner, flags, post0, post1, lo, hi,
    plo, phi, clo, chi, ulo, uhi, ux, uy, uz, wx, wl, wy, wz, ax, al, ay, az, inv,
    load_sem, small_sem, own_sem,
    send_sem, recv_sem, psend, precv, csend, crecv, usend, urecv, asend, arecv,
):
    posts, concs = (post0, post1), (conc0, conc1)
    w, n = lax.axis_index("wide"), lax.axis_index("narrow")
    chunks = narrow
    per_chunk = tile // B
    parts = PARTS
    part = width // parts
    strip = w * narrow + n

    def neighbour(offset):
        g = lax.rem(strip + offset + wide * narrow, wide * narrow)
        return (g // narrow, lax.rem(g, narrow))

    after, before = neighbour(1), neighbour(-1)
    first, last = strip == 0, strip == wide * narrow - 1

    barrier = pltpu.get_barrier_semaphore()
    pl.semaphore_signal(barrier, inc=1, device_id=after, device_id_type=MESH)
    pl.semaphore_signal(barrier, inc=1, device_id=before, device_id_type=MESH)
    for k in range(1, narrow):
        pl.semaphore_signal(
            barrier, inc=1, device_id=(w, lax.rem(n + k, narrow)), device_id_type=MESH
        )

    def part_cols(k):
        return pl.ds(pl.multiple_of(B + k * part, B), part)

    def cols(k):
        return pl.ds(pl.multiple_of(k * tile, tile), tile)

    def pcols(k):
        return pl.ds(pl.multiple_of(B + k * tile, B), tile)

    def load(k):
        return pltpu.make_async_copy(
            pop_in.at[:, :, :, cols(k)], fbuf.at[:, :, :, cols(k)], load_sem.at[k]
        )

    smalls = [
        pltpu.make_async_copy(phase_in, phase, small_sem.at[0]),
        pltpu.make_async_copy(poro_in, poro.at[:, :, pl.ds(B, width)], small_sem.at[1]),
        pltpu.make_async_copy(conc_in, conc0.at[:, :, pl.ds(B, width)], small_sem.at[2]),
        pltpu.make_async_copy(napl_in, napl, small_sem.at[3]),
        pltpu.make_async_copy(flags_in, flags, small_sem.at[4]),
    ]
    smalls[0].start()
    load(0).start()
    for copy in smalls[1:]:
        copy.start()
    for k in range(1, chunks):
        load(k).start()

    lane = lax.broadcasted_iota(jnp.int32, (R, B), 1)
    row = lax.broadcasted_iota(jnp.int32, (R, B), 0)
    nan = jnp.full((R, B), jnp.nan, jnp.float32)
    zero = jnp.zeros((R, B), jnp.float32)
    ends = (pl.ds(0, B), pl.ds(B + width, B))

    def fill(z, carry):
        for end in ends:
            for p in range(2):
                for q in range(19):
                    if DIRS[q][1]:
                        posts[p][SLOT[q], z, :, end] = nan
            for s in range(STEPS):
                for m in (1, 2):
                    lo[s, m, z, :, end] = nan
                    hi[s, m, z, :, end] = nan
            poro[z, :, end] = zero
            uy[z, :, end] = zero
            for p in range(2):
                concs[p][z, :, end] = zero
        return carry

    lax.fori_loop(0, Z, fill, 0)

    def edge(s, side, k):
        post = posts[s % 2]
        if side == 0:
            src = post.at[pl.ds(0, 5), :, pl.ds(R - 1, 1), part_cols(k)]
            dst = lo.at[s, :, :, pl.ds(R - 1, 1), part_cols(k)]
        else:
            src = post.at[pl.ds(5, 5), :, pl.ds(0, 1), part_cols(k)]
            dst = hi.at[s, :, :, pl.ds(0, 1), part_cols(k)]
        return pltpu.make_async_remote_copy(
            src_ref=src, dst_ref=dst, send_sem=send_sem.at[s, side, k], recv_sem=recv_sem.at[s, side, k],
            device_id=after if side == 0 else before, device_id_type=MESH,
        )

    def poro_edge(side):
        rows = pl.ds(R - 1, 1) if side == 0 else pl.ds(0, 1)
        inner = pl.ds(B, width)
        return pltpu.make_async_remote_copy(
            src_ref=poro.at[:, rows, inner], dst_ref=(plo if side == 0 else phi).at[:, rows, :],
            send_sem=psend.at[side], recv_sem=precv.at[side],
            device_id=after if side == 0 else before, device_id_type=MESH,
        )

    def conc_edge(p, side, k):
        rows = pl.ds(R - 2, 2) if side == 0 else pl.ds(0, 2)
        src, dst = (pl.ds(B, width), pl.ds(0, width)) if p == 0 else (pcols(k), cols(k))
        return pltpu.make_async_remote_copy(
            src_ref=concs[p].at[:, rows, src], dst_ref=(clo if side == 0 else chi).at[p, :, rows, dst],
            send_sem=csend.at[p, side, k], recv_sem=crecv.at[p, side, k],
            device_id=after if side == 0 else before, device_id_type=MESH,
        )

    def vel_edge(side, k):
        rows = pl.ds(R - 1, 1) if side == 0 else pl.ds(0, 1)
        return pltpu.make_async_remote_copy(
            src_ref=ux.at[:, rows, cols(k)], dst_ref=(ulo if side == 0 else uhi).at[:, rows, cols(k)],
            send_sem=usend.at[side, k], recv_sem=urecv.at[side, k],
            device_id=after if side == 0 else before, device_id_type=MESH,
        )

    def start_open(side, copy):
        pl.when(jnp.logical_not(last if side == 0 else first))(copy.start)

    def sent_open(side, copy):
        pl.when(jnp.logical_not(last if side == 0 else first))(copy.wait_send)

    def await_open(side, copy):
        pl.when(jnp.logical_not(first if side == 0 else last))(copy.wait_recv)

    def to_tile(a, k):
        src, dst = (napl2, napl_out) if a == 0 else (conc2, conc_out)
        rows = pl.ds(pl.multiple_of(n * R, R), R)
        return pltpu.make_async_remote_copy(
            src_ref=src.at[:, :, cols(k)], dst_ref=dst.at[:, rows, :],
            send_sem=asend.at[a, k], recv_sem=arecv.at[a, n], device_id=(w, k), device_id_type=MESH,
        )

    def from_tile(a, k):
        src, dst = (napl2, napl_out) if a == 0 else (conc2, conc_out)
        rows = pl.ds(pl.multiple_of(k * R, R), R)
        return pltpu.make_async_remote_copy(
            src_ref=src.at[:, :, cols(k)], dst_ref=dst.at[:, rows, :],
            send_sem=asend.at[a, k], recv_sem=arecv.at[a, k], device_id=(w, k), device_id_type=MESH,
        )

    def own_tile(a):
        src, dst = (napl2, napl_out) if a == 0 else (conc2, conc_out)
        rows = pl.ds(pl.multiple_of(n * R, R), R)
        return pltpu.make_async_copy(src.at[:, :, cols(n)], dst.at[:, rows, :], own_sem.at[a])

    def send_tile(a, k):
        @pl.when(k != n)
        def _():
            to_tile(a, k).start()

        @pl.when(k == n)
        def _():
            own_tile(a).start()

    def blocks(k, fn, carry=0, count=per_chunk):
        return lax.fori_loop(0, count, lambda i, c: fn(k * count + i, c), carry, unroll=True)

    def at(b):
        return pl.ds(pl.multiple_of(b * B, B), B)

    def start_block(b, carry):
        here, there = at(b), at(b + 1)
        for z in range(Z):
            f = [fbuf[q, z, :, here] for q in range(19)]
            out = collide(f, phase[z, :, here])
            for q in range(19):
                post0[SLOT[q], z, :, there] = out[q]
        return carry

    per_part, ratio = part // B, parts // chunks
    smalls[0].wait()
    load(0).wait()
    blocks(0, start_block, 0, per_part)
    pl.semaphore_wait(barrier, narrow + 1)
    for side in range(2):
        edge(0, side, 0).start()

    def first_part(k, carry):
        @pl.when(lax.rem(k, ratio) == 0)
        def _():
            load(k // ratio).wait()

        blocks(k, start_block, 0, per_part)
        for side in range(2):
            edge(0, side, k).start()
        return carry

    lax.fori_loop(1, parts, first_part, 0)
    for copy in smalls[1:]:
        copy.wait()
    def each_block(fn):
        def one(b, carry):
            for z in range(Z):
                fn(z, at(b), at(b + 1))
            return carry

        lax.fori_loop(0, width // B, one, 0)

    def inlet(z, here, there):
        plo[z, :, here] = jnp.broadcast_to(flags[0, z : z + 1, here].astype(jnp.float32), (R, B))
        for p in range(2):
            clo[p, z, :, here] = zero

    def outlet(z, here, there):
        phi[z, :, here] = jnp.broadcast_to(flags[1, z : z + 1, here].astype(jnp.float32), (R, B))

    def outlet_conc(p):
        def fill_rows(z, here, there):
            own = concs[p][z, :, there]
            chi[p, z, :, here] = jnp.where(row == 0, pltpu.roll(own, 1, 0), pltpu.roll(own, 2, 0))

        pl.when(last)(lambda: each_block(fill_rows))

    def inlet_vel(z, here, there):
        ulo[z, :, here] = pltpu.roll(ux[z, :, here], R - 1, 0)

    def outlet_vel(z, here, there):
        uhi[z, :, here] = pltpu.roll(ux[z, :, here], 1, 0)

    pl.when(first)(lambda: each_block(inlet))
    pl.when(last)(lambda: each_block(outlet))
    outlet_conc(0)
    for side in range(2):
        start_open(side, poro_edge(side))

    def stream(post, s, z, b):
        base = b * B + B

        def block(slot, layer, shift, ex):
            where = pl.ds(pl.multiple_of(base + shift, B), B)
            value = post[slot, layer, :, where]
            if ex == 1:
                value = jnp.where(row == R - 1, lo[s, slot, layer, :, where], value)
            elif ex == -1:
                value = jnp.where(row == 0, hi[s, slot - 5, layer, :, where], value)
            return value

        here = pl.ds(pl.multiple_of(base, B), B)
        f = []
        for q in range(19):
            ex, ey, ez = DIRS[q]
            slot, layer = SLOT[q], (z - ez) % Z
            if q == 0:
                f.append(post[slot, z, :, here])
                continue
            moved = block(slot, layer, 0, ex)
            if ey == 1:
                moved = pltpu.roll(jnp.where(lane == B - 1, block(slot, layer, -B, ex), moved), 1, 1)
            elif ey == -1:
                moved = pltpu.roll(jnp.where(lane == 0, block(slot, layer, B, ex), moved), B - 1, 1)
            if ex:
                moved = pltpu.roll(moved, 1 if ex == 1 else R - 1, 0)
            f.append(jnp.where(moved < jnp.inf, moved, post[SLOT[OPP[q]], z, :, here]))
        return f

    def await_edges(s, k):
        @pl.when(k == 0)
        def _():
            for side in range(2):
                edge(s, side, k).wait_recv()

        @pl.when(k < parts - 1)
        def _():
            for side in range(2):
                edge(s, side, k + 1).wait_recv()

    def one_step(s):
        old, new = posts[(s + 1) % 2], posts[s % 2]

        def move_block(b, c):
            for z in range(Z):
                out = collide(stream(old, s - 1, z, b), phase[z, :, at(b)])
                for q in range(19):
                    new[SLOT[q], z, :, at(b + 1)] = out[q]
            return c

        def chunk(k, c):
            await_edges(s - 1, k)

            if s >= 2:
                for side in range(2):
                    edge(s - 2, side, k).wait_send()

            blocks(k, move_block, 0, per_part)
            for side in range(2):
                edge(s, side, k).start()
            return c

        lax.fori_loop(0, parts, chunk, 0)

        if s == 1:
            for side in range(2):
                start_open(side, conc_edge(0, side, 0))
        if s == 2:
            for side in range(2):
                await_open(side, poro_edge(side))

            def coef(b, c):
                here, there, beyond = at(b), at(b + 1), at(b + 2)
                for z in range(Z):
                    own = poro[z, :, there]
                    high, low = phi[z, :, here], plo[z, :, here]
                    wx[z, :, here] = own * pltpu.roll(jnp.where(row == 0, high, own), R - 1, 0)
                    wl[z, :, here] = low * pltpu.roll(own, R - 1, 0)
                    wy[z, :, here] = own * pltpu.roll(jnp.where(lane == 0, poro[z, :, beyond], own), B - 1, 1)
                    wz[z, :, here] = own * poro[(z + 1) % Z, :, there]
                    inv[z, :, here] = 1.0 / jnp.maximum(own, 0.3)
                return c

            lax.fori_loop(0, width // B, coef, 0, unroll=2)

    for s in range(1, STEPS):
        one_step(s)

    def last_block(b, carry):
        here, there = at(b), at(b + 1)
        for z in range(Z):
            f = stream(posts[(STEPS - 1) % 2], STEPS - 1, z, b)
            solid = phase[z, :, here] == 2
            rho, jx, jy, jz = moments(f)
            per = jnp.where(solid, 0.0, 1.0) / jnp.where(solid, 1.0, rho)
            ux[z, :, here] = jnp.where(solid, 0.0, jx * per)
            uy[z, :, there] = jnp.where(solid, 0.0, jy * per)
            uz[z, :, here] = jnp.where(solid, 0.0, jz * per)
            for q in range(19):
                pop_out[q, z, :, here] = jnp.where(solid, fbuf[q, z, :, here], f[q])
        return carry

    def last_part(k, carry):
        await_edges(STEPS - 1, k)
        blocks(k, last_block, 0, per_part)

        @pl.when(lax.rem(k, ratio) == ratio - 1)
        def _():
            for side in range(2):
                start_open(side, vel_edge(side, k // ratio))

        return carry

    lax.fori_loop(0, parts, last_part, 0)

    def inner_flux(step, b, carry):
        here, there, back, beyond = at(b), at(b + 1), at(b), at(b + 2)
        conc = concs[step]
        c = [conc[z, :, there] for z in range(Z)]
        if step == 0:
            for z in range(Z):
                vy = uy[z, :, there]
                ay[z, :, here] = wy[z, :, here] * (
                    0.5 * (vy + pltpu.roll(jnp.where(lane == 0, uy[z, :, beyond], vy), B - 1, 1))
                )
                az[z, :, here] = wz[z, :, here] * (0.5 * (uz[z, :, here] + uz[(z + 1) % Z, :, here]))
        zflux = [
            face_flux(
                c[(z - 1) % Z], c[z], c[(z + 1) % Z], c[(z + 2) % Z], wz[z, :, here], az[z, :, here]
            )
            for z in range(Z)
        ]
        flow = []
        for z in range(Z):
            own = c[z]
            cb, cn = conc[z, :, back], conc[z, :, beyond]
            left = pltpu.roll(jnp.where(lane == B - 1, cb, own), 1, 1)
            right = pltpu.roll(jnp.where(lane == 0, cn, own), B - 1, 1)
            right2 = pltpu.roll(jnp.where(lane < 2, cn, own), B - 2, 1)
            yflux = face_flux(left, own, right, right2, wy[z, :, here], ay[z, :, here])
            flow.append(yflux)
            change = pltpu.roll(jnp.where(lane == B - 1, carry[z], yflux), 1, 1) - yflux
            inner[z, :, here] = change + (zflux[(z - 1) % Z] - zflux[z])
        return tuple(flow)

    def transport(step, b, carry):
        here, there = at(b), at(b + 1)
        conc = concs[step]
        for z in range(Z):
            own = conc[z, :, there]
            high = chi[step, z, :, here]
            low = clo[step, z, :, here]
            if step == 0:
                vx = ux[z, :, here]
                nxt = pltpu.roll(jnp.where(row == 0, uhi[z, :, here], vx), R - 1, 0)
                a = wx[z, :, here] * (0.5 * (vx + nxt))
                e = wl[z, :, here] * (0.5 * (ulo[z, :, here] + pltpu.roll(vx, R - 1, 0)))
                ax[z, :, here] = a
                al[z, :, here] = e
            else:
                a, e = ax[z, :, here], al[z, :, here]
            up1, up2 = pltpu.roll(own, R - 1, 0), pltpu.roll(own, R - 2, 0)
            down1 = pltpu.roll(jnp.where(row == R - 1, low, own), 1, 0)
            ahead = pltpu.roll(jnp.where(row == 0, high, own), R - 1, 0)
            far = pltpu.roll(jnp.where(row < 2, high, own), R - 2, 0)
            xflux = face_flux(down1, own, ahead, far, wx[z, :, here], a)
            xlow = face_flux(pltpu.roll(low, 1, 0), low, up1, up2, wl[z, :, here], e)
            change = pltpu.roll(jnp.where(row == R - 1, xlow, xflux), 1, 0) - xflux
            change = change + inner[z, :, here]
            if step == 0:
                s = napl[z, :, here]
                rate = 0.3 * s * (1.0 - own)
                new = own + (change + rate) * inv[z, :, here]
                conc1[z, :, there] = new
                s = s - 0.5 * rate
                rate = 0.3 * s * (1.0 - new)
                napl2[z, :, here] = s - 0.5 * rate
                rate_buf[z, :, here] = rate
            else:
                conc2[z, :, here] = own + (change + rate_buf[z, :, here]) * inv[z, :, here]
        return carry

    def first_transport(k, carry):
        for side in range(2):
            await_open(side, vel_edge(side, k))
        blocks(k, functools.partial(transport, 0))
        for side in range(2):
            start_open(side, conc_edge(1, side, k))
        send_tile(0, k)
        return carry

    def second_transport(k, carry):
        for side in range(2):
            await_open(side, conc_edge(1, side, k))
        blocks(k, functools.partial(transport, 1))
        send_tile(1, k)
        return carry

    still = (zero,) * Z
    lax.fori_loop(0, width // B, functools.partial(inner_flux, 0), still, unroll=4)
    for side in range(2):
        await_open(side, conc_edge(0, side, 0))
    pl.when(first)(lambda: each_block(inlet_vel))
    pl.when(last)(lambda: each_block(outlet_vel))
    lax.fori_loop(0, chunks, first_transport, 0)
    outlet_conc(1)
    lax.fori_loop(0, width // B, functools.partial(inner_flux, 1), still, unroll=4)
    lax.fori_loop(0, chunks, second_transport, 0)

    def settle_part(k, carry):
        for side in range(2):
            for s in (STEPS - 2, STEPS - 1):
                edge(s, side, k).wait_send()
        return carry

    def settle(k, carry):
        for side in range(2):
            sent_open(side, vel_edge(side, k))
            sent_open(side, conc_edge(1, side, k))
        return carry

    lax.fori_loop(0, parts, settle_part, 0)
    lax.fori_loop(0, chunks, settle, 0)
    for side in range(2):
        sent_open(side, poro_edge(side))
        sent_open(side, conc_edge(0, side, 0))

    def settle_tile(k, carry):
        @pl.when(k != n)
        def _():
            for a in range(2):
                to_tile(a, k).wait_send()
                from_tile(a, k).wait_recv()

        return carry

    lax.fori_loop(0, chunks, settle_tile, 0)
    for a in range(2):
        own_tile(a).wait()


def local(wide, narrow, populations, phase, porosity, napl, concentration, flags):
    width = phase.shape[2]
    tile = width // narrow
    padded = width + 2 * B
    f32 = jnp.float32
    DMA = pltpu.SemaphoreType.DMA

    def full():
        return pltpu.VMEM((Z, R, width), f32)

    any_space = pl.BlockSpec(memory_space=pl.ANY)
    scratch = [
        pltpu.VMEM((19, Z, R, width), f32),
        pltpu.VMEM((Z, R, width), jnp.int32),
        pltpu.VMEM((Z, R, padded), f32),
        full(),
        pltpu.VMEM((Z, R, padded), f32), pltpu.VMEM((Z, R, padded), f32),
        full(), full(), full(), full(),
        pltpu.VMEM((2, Z, width), jnp.int32),
        pltpu.VMEM((19, Z, R, padded), f32), pltpu.VMEM((19, Z, R, padded), f32),
        pltpu.VMEM((STEPS, 5, Z, R, padded), f32),
        pltpu.VMEM((STEPS, 5, Z, R, padded), f32),
        full(), full(),
        pltpu.VMEM((2, Z, R, width), f32), pltpu.VMEM((2, Z, R, width), f32),
        full(), full(),
        full(), pltpu.VMEM((Z, R, padded), f32), full(),
        full(), full(), full(), full(),
        full(), full(), full(), full(),
        full(),
        DMA((narrow,)), DMA((5,)), DMA((2,)),
        DMA((STEPS, 2, PARTS)), DMA((STEPS, 2, PARTS)),
        DMA((2,)), DMA((2,)),
        DMA((2, 2, narrow)), DMA((2, 2, narrow)),
        DMA((2, narrow)), DMA((2, narrow)),
        DMA((2, narrow)), DMA((2, narrow)),
    ]
    tiles = jax.ShapeDtypeStruct((Z, R * narrow, tile), f32)
    return pl.pallas_call(
        functools.partial(body, wide, narrow, width, tile),
        out_shape=(pltpu.VMEM(populations.shape, f32),) + (pltpu.VMEM(tiles.shape, f32),) * 2,
        in_specs=[any_space] * 6,
        out_specs=(pl.BlockSpec(memory_space=pltpu.VMEM),) * 3,
        scratch_shapes=scratch,
        compiler_params=pltpu.CompilerParams(
            collective_id=0, has_side_effects=True, vmem_limit_bytes=56 * 2**20
        ),
        name="dissolution",
    )(populations, phase, porosity, napl, concentration, flags)


def solution(mesh):
    strips = ("wide", "narrow")
    in_specs = (
        P(None, None, strips, None),
        P(None, strips, None),
        P(None, strips, None),
        P(None, strips, None),
        P(None, strips, None),
        P(),
    )
    out_specs = (
        P(None, None, strips, None),
        P(None, "wide", "narrow"),
        P(None, "wide", "narrow"),
    )
    fn = functools.partial(local, mesh.shape["wide"], mesh.shape["narrow"])
    return jax.shard_map(fn, mesh=mesh, in_specs=in_specs, out_specs=out_specs, check_vma=False)
```

```python
import functools

import jax
import jax.numpy as jnp
from jax import lax
from jax.experimental import pallas as pl
from jax.experimental.pallas import tpu as pltpu
from jax.sharding import PartitionSpec as P

MESH = pl.DeviceIdType.MESH
DIRS = [
    (0, 0, 0), (1, 0, 0), (-1, 0, 0), (0, 1, 0), (0, -1, 0), (0, 0, 1), (0, 0, -1),
    (1, 1, 0), (-1, -1, 0), (1, -1, 0), (-1, 1, 0), (1, 0, 1), (-1, 0, -1), (1, 0, -1), (-1, 0, 1),
    (0, 1, 1), (0, -1, -1), (0, 1, -1), (0, -1, 1),
]
OPP = [0, 2, 1, 4, 3, 6, 5, 8, 7, 10, 9, 12, 11, 14, 13, 16, 15, 18, 17]
UP = [1, 7, 9, 11, 13]
DOWN = [2, 8, 10, 12, 14]
ORDER = UP + DOWN + [0, 3, 4, 5, 6, 15, 16, 17, 18]
SLOT = {q: i for i, q in enumerate(ORDER)}
STEPS = 4
PARTS = 16
Z = 4
R = 8
B = 128


def collide(f, phase):
    total, diff = {}, {}
    for q in range(1, 19, 2):
        total[q] = f[q] + f[q + 1]
        diff[q] = f[q] - f[q + 1]
    rho = (
        ((f[0] + total[1]) + (total[3] + total[5]))
        + ((total[7] + total[9]) + (total[11] + total[13]))
        + (total[15] + total[17])
    )
    jx = (diff[1] + diff[7]) + (diff[9] + diff[11]) + diff[13]
    jy = (diff[3] + diff[7]) + (diff[15] - diff[9]) + diff[17]
    jz = (diff[5] + diff[11]) + (diff[15] - diff[13]) - diff[17]
    rho = jnp.where(phase == 2, jnp.nan, rho)
    factor = jnp.where(phase == 1, 0.5, 1.0)
    per = factor / rho
    vx, vy, vz = jx * per, jy * per, jz * per
    factor = factor * (3.75 / 36.0)
    nx, ny, nz = jx * factor, jy * factor, jz * factor
    hx, hy, hz = vx * 1.5, vy * 1.5, vz * 1.5
    sxx, syy, szz = nx * hx, ny * hy, nz * hz
    hx, hy = hx + hx, hy + hy
    xy, xz, yz = ny * hx, nz * hx, nz * hy
    even = rho * (1.25 / 36.0) - (sxx + syy + szz) * (1.0 / 3.0)
    post = [None] * 19
    post[0] = 12.0 * even - 0.25 * f[0]

    def pair(q, e, o):
        post[q] = (e + o) - 0.25 * f[q]
        post[q + 1] = (e - o) - 0.25 * f[q + 1]

    ex, ey, ez = even + sxx, even + syy, even + szz
    pair(1, ex + ex, nx + nx)
    pair(3, ey + ey, ny + ny)
    pair(5, ez + ez, nz + nz)
    exy, exz, eyz = ex + syy, ex + szz, ey + szz
    pair(7, exy + xy, nx + ny)
    pair(9, exy - xy, nx - ny)
    pair(11, exz + xz, nx + nz)
    pair(13, exz - xz, nx - nz)
    pair(15, eyz + yz, ny + nz)
    pair(17, eyz - yz, ny - nz)
    return post


def moments(f):
    total, diff = {}, {}
    for q in range(1, 19, 2):
        total[q] = f[q] + f[q + 1]
        diff[q] = f[q] - f[q + 1]
    rho = (
        ((f[0] + total[1]) + (total[3] + total[5]))
        + ((total[7] + total[9]) + (total[11] + total[13]))
        + (total[15] + total[17])
    )
    jx = (diff[1] + diff[7]) + (diff[9] + diff[11]) + diff[13]
    jy = (diff[3] + diff[7]) + (diff[15] - diff[9]) + diff[17]
    jz = (diff[5] + diff[11]) + (diff[15] - diff[13]) - diff[17]
    return rho, jx, jy, jz


def half_minmod(p, q):
    return 0.5 * jnp.maximum(jnp.minimum(p, q), jnp.minimum(jnp.maximum(p, q), 0.0))


def face_flux(back, here, ahead, far, w, a):
    step = ahead - here
    up = here + half_minmod(here - back, step)
    down = ahead - half_minmod(step, far - ahead)
    return a * jnp.where(a > 0, up, down) - (0.15 * w) * step


def body(
    wide, narrow, width, tile,
    pop_in, phase_in, poro_in, napl_in, conc_in, flags_in,
    pop_out, conc_out, napl_out,
    fbuf, phase, poro, napl, conc0, conc1, conc2, napl2, rate_buf, inner, flags, post0, post1, lo, hi,
    plo, phi, clo, chi, ulo, uhi, ux, uy, uz, wx, wl, wy, wz, ax, al, ay, az, inv,
    load_sem, small_sem, own_sem,
    send_sem, recv_sem, psend, precv, csend, crecv, usend, urecv, asend, arecv,
):
    posts, concs = (post0, post1), (conc0, conc1)
    w, n = lax.axis_index("wide"), lax.axis_index("narrow")
    chunks = narrow
    per_chunk = tile // B
    parts = PARTS
    part = width // parts
    strip = w * narrow + n

    def neighbour(offset):
        g = lax.rem(strip + offset + wide * narrow, wide * narrow)
        return (g // narrow, lax.rem(g, narrow))

    after, before = neighbour(1), neighbour(-1)
    first, last = strip == 0, strip == wide * narrow - 1

    barrier = pltpu.get_barrier_semaphore()
    pl.semaphore_signal(barrier, inc=1, device_id=after, device_id_type=MESH)
    pl.semaphore_signal(barrier, inc=1, device_id=before, device_id_type=MESH)
    for k in range(1, narrow):
        pl.semaphore_signal(
            barrier, inc=1, device_id=(w, lax.rem(n + k, narrow)), device_id_type=MESH
        )

    def part_cols(k):
        return pl.ds(pl.multiple_of(B + k * part, B), part)

    def cols(k):
        return pl.ds(pl.multiple_of(k * tile, tile), tile)

    def pcols(k):
        return pl.ds(pl.multiple_of(B + k * tile, B), tile)

    def load(k):
        return pltpu.make_async_copy(
            pop_in.at[:, :, :, cols(k)], fbuf.at[:, :, :, cols(k)], load_sem.at[k]
        )

    smalls = [
        pltpu.make_async_copy(phase_in, phase, small_sem.at[0]),
        pltpu.make_async_copy(poro_in, poro.at[:, :, pl.ds(B, width)], small_sem.at[1]),
        pltpu.make_async_copy(conc_in, conc0.at[:, :, pl.ds(B, width)], small_sem.at[2]),
        pltpu.make_async_copy(napl_in, napl, small_sem.at[3]),
        pltpu.make_async_copy(flags_in, flags, small_sem.at[4]),
    ]
    smalls[0].start()
    load(0).start()
    for k in range(1, chunks):
        load(k).start()
    for copy in smalls[1:]:
        copy.start()

    lane = lax.broadcasted_iota(jnp.int32, (R, B), 1)
    row = lax.broadcasted_iota(jnp.int32, (R, B), 0)
    nan = jnp.full((R, B), jnp.nan, jnp.float32)
    zero = jnp.zeros((R, B), jnp.float32)
    ends = (pl.ds(0, B), pl.ds(B + width, B))

    def fill(z, carry):
        for end in ends:
            for p in range(2):
                for q in range(19):
                    if DIRS[q][1]:
                        posts[p][SLOT[q], z, :, end] = nan
            for s in range(STEPS):
                for m in (1, 2):
                    lo[s, m, z, :, end] = nan
                    hi[s, m, z, :, end] = nan
            poro[z, :, end] = zero
            uy[z, :, end] = zero
            for p in range(2):
                concs[p][z, :, end] = zero
        return carry

    def edge(s, side, k):
        post = posts[s % 2]
        if side == 0:
            src = post.at[pl.ds(0, 5), :, pl.ds(R - 1, 1), part_cols(k)]
            dst = lo.at[s, :, :, pl.ds(R - 1, 1), part_cols(k)]
        else:
            src = post.at[pl.ds(5, 5), :, pl.ds(0, 1), part_cols(k)]
            dst = hi.at[s, :, :, pl.ds(0, 1), part_cols(k)]
        return pltpu.make_async_remote_copy(
            src_ref=src, dst_ref=dst, send_sem=send_sem.at[s, side, k], recv_sem=recv_sem.at[s, side, k],
            device_id=after if side == 0 else before, device_id_type=MESH,
        )

    def poro_edge(side):
        rows = pl.ds(R - 1, 1) if side == 0 else pl.ds(0, 1)
        inner = pl.ds(B, width)
        return pltpu.make_async_remote_copy(
            src_ref=poro.at[:, rows, inner], dst_ref=(plo if side == 0 else phi).at[:, rows, :],
            send_sem=psend.at[side], recv_sem=precv.at[side],
            device_id=after if side == 0 else before, device_id_type=MESH,
        )

    def conc_edge(p, side, k):
        rows = pl.ds(R - 2, 2) if side == 0 else pl.ds(0, 2)
        src, dst = (pl.ds(B, width), pl.ds(0, width)) if p == 0 else (pcols(k), cols(k))
        return pltpu.make_async_remote_copy(
            src_ref=concs[p].at[:, rows, src], dst_ref=(clo if side == 0 else chi).at[p, :, rows, dst],
            send_sem=csend.at[p, side, k], recv_sem=crecv.at[p, side, k],
            device_id=after if side == 0 else before, device_id_type=MESH,
        )

    def vel_edge(side, k):
        rows = pl.ds(R - 1, 1) if side == 0 else pl.ds(0, 1)
        return pltpu.make_async_remote_copy(
            src_ref=ux.at[:, rows, cols(k)], dst_ref=(ulo if side == 0 else uhi).at[:, rows, cols(k)],
            send_sem=usend.at[side, k], recv_sem=urecv.at[side, k],
            device_id=after if side == 0 else before, device_id_type=MESH,
        )

    def start_open(side, copy):
        pl.when(jnp.logical_not(last if side == 0 else first))(copy.start)

    def sent_open(side, copy):
        pl.when(jnp.logical_not(last if side == 0 else first))(copy.wait_send)

    def await_open(side, copy):
        pl.when(jnp.logical_not(first if side == 0 else last))(copy.wait_recv)

    def to_tile(a, k):
        src, dst = (napl2, napl_out) if a == 0 else (conc2, conc_out)
        rows = pl.ds(pl.multiple_of(n * R, R), R)
        return pltpu.make_async_remote_copy(
            src_ref=src.at[:, :, cols(k)], dst_ref=dst.at[:, rows, :],
            send_sem=asend.at[a, k], recv_sem=arecv.at[a, n], device_id=(w, k), device_id_type=MESH,
        )

    def from_tile(a, k):
        src, dst = (napl2, napl_out) if a == 0 else (conc2, conc_out)
        rows = pl.ds(pl.multiple_of(k * R, R), R)
        return pltpu.make_async_remote_copy(
            src_ref=src.at[:, :, cols(k)], dst_ref=dst.at[:, rows, :],
            send_sem=asend.at[a, k], recv_sem=arecv.at[a, k], device_id=(w, k), device_id_type=MESH,
        )

    def own_tile(a):
        src, dst = (napl2, napl_out) if a == 0 else (conc2, conc_out)
        rows = pl.ds(pl.multiple_of(n * R, R), R)
        return pltpu.make_async_copy(src.at[:, :, cols(n)], dst.at[:, rows, :], own_sem.at[a])

    def send_tile(a, k):
        @pl.when(k != n)
        def _():
            to_tile(a, k).start()

        @pl.when(k == n)
        def _():
            own_tile(a).start()

    def blocks(k, fn, carry=0, count=per_chunk):
        return lax.fori_loop(0, count, lambda i, c: fn(k * count + i, c), carry, unroll=True)

    def at(b):
        return pl.ds(pl.multiple_of(b * B, B), B)

    def start_block(b, carry):
        here, there = at(b), at(b + 1)
        for z in range(Z):
            f = [fbuf[q, z, :, here] for q in range(19)]
            out = collide(f, phase[z, :, here])
            for q in range(19):
                post0[SLOT[q], z, :, there] = out[q]
        return carry

    per_part, ratio = part // B, parts // chunks
    smalls[0].wait()
    load(0).wait()
    blocks(0, start_block, 0, per_part)
    pl.semaphore_wait(barrier, narrow + 1)
    for side in range(2):
        edge(0, side, 0).start()

    def first_part(k, carry):
        @pl.when(lax.rem(k, ratio) == 0)
        def _():
            load(k // ratio).wait()

        blocks(k, start_block, 0, per_part)
        for side in range(2):
            edge(0, side, k).start()
        return carry

    lax.fori_loop(1, parts, first_part, 0)
    lax.fori_loop(0, Z, fill, 0)
    for copy in smalls[1:]:
        copy.wait()
    def each_block(fn):
        def one(b, carry):
            for z in range(Z):
                fn(z, at(b), at(b + 1))
            return carry

        lax.fori_loop(0, width // B, one, 0)

    def inlet(z, here, there):
        plo[z, :, here] = jnp.broadcast_to(flags[0, z : z + 1, here].astype(jnp.float32), (R, B))
        for p in range(2):
            clo[p, z, :, here] = zero

    def outlet(z, here, there):
        phi[z, :, here] = jnp.broadcast_to(flags[1, z : z + 1, here].astype(jnp.float32), (R, B))

    def outlet_conc(p):
        def fill_rows(z, here, there):
            own = concs[p][z, :, there]
            chi[p, z, :, here] = jnp.where(row == 0, pltpu.roll(own, 1, 0), pltpu.roll(own, 2, 0))

        pl.when(last)(lambda: each_block(fill_rows))

    def inlet_vel(z, here, there):
        ulo[z, :, here] = pltpu.roll(ux[z, :, here], R - 1, 0)

    def outlet_vel(z, here, there):
        uhi[z, :, here] = pltpu.roll(ux[z, :, here], 1, 0)

    pl.when(first)(lambda: each_block(inlet))
    pl.when(last)(lambda: each_block(outlet))
    outlet_conc(0)
    for side in range(2):
        start_open(side, poro_edge(side))

    def stream(post, s, z, b):
        base = b * B + B

        def block(slot, layer, shift, ex):
            where = pl.ds(pl.multiple_of(base + shift, B), B)
            value = post[slot, layer, :, where]
            if ex == 1:
                value = jnp.where(row == R - 1, lo[s, slot, layer, :, where], value)
            elif ex == -1:
                value = jnp.where(row == 0, hi[s, slot - 5, layer, :, where], value)
            return value

        here = pl.ds(pl.multiple_of(base, B), B)
        f = []
        for q in range(19):
            ex, ey, ez = DIRS[q]
            slot, layer = SLOT[q], (z - ez) % Z
            if q == 0:
                f.append(post[slot, z, :, here])
                continue
            moved = block(slot, layer, 0, ex)
            if ey == 1:
                moved = pltpu.roll(jnp.where(lane == B - 1, block(slot, layer, -B, ex), moved), 1, 1)
            elif ey == -1:
                moved = pltpu.roll(jnp.where(lane == 0, block(slot, layer, B, ex), moved), B - 1, 1)
            if ex:
                moved = pltpu.roll(moved, 1 if ex == 1 else R - 1, 0)
            f.append(jnp.where(moved < jnp.inf, moved, post[SLOT[OPP[q]], z, :, here]))
        return f

    def await_edges(s, k):
        @pl.when(k == 0)
        def _():
            for side in range(2):
                edge(s, side, k).wait_recv()

        @pl.when(k < parts - 1)
        def _():
            for side in range(2):
                edge(s, side, k + 1).wait_recv()

    def one_step(s):
        old, new = posts[(s + 1) % 2], posts[s % 2]

        def move_block(b, c):
            for z in range(Z):
                out = collide(stream(old, s - 1, z, b), phase[z, :, at(b)])
                for q in range(19):
                    new[SLOT[q], z, :, at(b + 1)] = out[q]
            return c

        def chunk(k, c):
            await_edges(s - 1, k)

            if s >= 2:
                for side in range(2):
                    edge(s - 2, side, k).wait_send()

            blocks(k, move_block, 0, per_part)
            for side in range(2):
                edge(s, side, k).start()
            return c

        lax.fori_loop(0, parts, chunk, 0)

        if s == 1:
            for side in range(2):
                start_open(side, conc_edge(0, side, 0))
        if s == 2:
            for side in range(2):
                await_open(side, poro_edge(side))

            def coef(b, c):
                here, there, beyond = at(b), at(b + 1), at(b + 2)
                for z in range(Z):
                    own = poro[z, :, there]
                    high, low = phi[z, :, here], plo[z, :, here]
                    wx[z, :, here] = own * pltpu.roll(jnp.where(row == 0, high, own), R - 1, 0)
                    wl[z, :, here] = low * pltpu.roll(own, R - 1, 0)
                    wy[z, :, here] = own * pltpu.roll(jnp.where(lane == 0, poro[z, :, beyond], own), B - 1, 1)
                    wz[z, :, here] = own * poro[(z + 1) % Z, :, there]
                    inv[z, :, here] = 1.0 / jnp.maximum(own, 0.3)
                return c

            lax.fori_loop(0, width // B, coef, 0, unroll=2)

    for s in range(1, STEPS):
        one_step(s)

    def last_block(b, carry):
        here, there = at(b), at(b + 1)
        for z in range(Z):
            f = stream(posts[(STEPS - 1) % 2], STEPS - 1, z, b)
            solid = phase[z, :, here] == 2
            rho, jx, jy, jz = moments(f)
            per = jnp.where(solid, 0.0, 1.0) / jnp.where(solid, 1.0, rho)
            ux[z, :, here] = jnp.where(solid, 0.0, jx * per)
            uy[z, :, there] = jnp.where(solid, 0.0, jy * per)
            uz[z, :, here] = jnp.where(solid, 0.0, jz * per)
            for q in range(19):
                pop_out[q, z, :, here] = jnp.where(solid, fbuf[q, z, :, here], f[q])
        return carry

    def last_part(k, carry):
        await_edges(STEPS - 1, k)
        blocks(k, last_block, 0, per_part)

        @pl.when(lax.rem(k, ratio) == ratio - 1)
        def _():
            for side in range(2):
                start_open(side, vel_edge(side, k // ratio))

        return carry

    lax.fori_loop(0, parts, last_part, 0)

    def inner_flux(step, b, carry):
        here, there, back, beyond = at(b), at(b + 1), at(b), at(b + 2)
        conc = concs[step]
        c = [conc[z, :, there] for z in range(Z)]
        if step == 0:
            for z in range(Z):
                vy = uy[z, :, there]
                ay[z, :, here] = wy[z, :, here] * (
                    0.5 * (vy + pltpu.roll(jnp.where(lane == 0, uy[z, :, beyond], vy), B - 1, 1))
                )
                az[z, :, here] = wz[z, :, here] * (0.5 * (uz[z, :, here] + uz[(z + 1) % Z, :, here]))
        zflux = [
            face_flux(
                c[(z - 1) % Z], c[z], c[(z + 1) % Z], c[(z + 2) % Z], wz[z, :, here], az[z, :, here]
            )
            for z in range(Z)
        ]
        flow = []
        for z in range(Z):
            own = c[z]
            cb, cn = conc[z, :, back], conc[z, :, beyond]
            left = pltpu.roll(jnp.where(lane == B - 1, cb, own), 1, 1)
            right = pltpu.roll(jnp.where(lane == 0, cn, own), B - 1, 1)
            right2 = pltpu.roll(jnp.where(lane < 2, cn, own), B - 2, 1)
            yflux = face_flux(left, own, right, right2, wy[z, :, here], ay[z, :, here])
            flow.append(yflux)
            change = pltpu.roll(jnp.where(lane == B - 1, carry[z], yflux), 1, 1) - yflux
            inner[z, :, here] = change + (zflux[(z - 1) % Z] - zflux[z])
        return tuple(flow)

    def transport(step, b, carry):
        here, there = at(b), at(b + 1)
        conc = concs[step]
        for z in range(Z):
            own = conc[z, :, there]
            high = chi[step, z, :, here]
            low = clo[step, z, :, here]
            if step == 0:
                vx = ux[z, :, here]
                nxt = pltpu.roll(jnp.where(row == 0, uhi[z, :, here], vx), R - 1, 0)
                a = wx[z, :, here] * (0.5 * (vx + nxt))
                e = wl[z, :, here] * (0.5 * (ulo[z, :, here] + pltpu.roll(vx, R - 1, 0)))
                ax[z, :, here] = a
                al[z, :, here] = e
            else:
                a, e = ax[z, :, here], al[z, :, here]
            up1, up2 = pltpu.roll(own, R - 1, 0), pltpu.roll(own, R - 2, 0)
            down1 = pltpu.roll(jnp.where(row == R - 1, low, own), 1, 0)
            ahead = pltpu.roll(jnp.where(row == 0, high, own), R - 1, 0)
            far = pltpu.roll(jnp.where(row < 2, high, own), R - 2, 0)
            xflux = face_flux(down1, own, ahead, far, wx[z, :, here], a)
            xlow = face_flux(pltpu.roll(low, 1, 0), low, up1, up2, wl[z, :, here], e)
            change = pltpu.roll(jnp.where(row == R - 1, xlow, xflux), 1, 0) - xflux
            change = change + inner[z, :, here]
            if step == 0:
                s = napl[z, :, here]
                rate = 0.3 * s * (1.0 - own)
                new = own + (change + rate) * inv[z, :, here]
                conc1[z, :, there] = new
                s = s - 0.5 * rate
                rate = 0.3 * s * (1.0 - new)
                napl2[z, :, here] = s - 0.5 * rate
                rate_buf[z, :, here] = rate
            else:
                conc2[z, :, here] = own + (change + rate_buf[z, :, here]) * inv[z, :, here]
        return carry

    def first_transport(k, carry):
        for side in range(2):
            await_open(side, vel_edge(side, k))
        blocks(k, functools.partial(transport, 0))
        for side in range(2):
            start_open(side, conc_edge(1, side, k))
        return carry

    def second_transport(k, carry):
        for side in range(2):
            await_open(side, conc_edge(1, side, k))
        blocks(k, functools.partial(transport, 1))
        send_tile(1, k)
        return carry

    def send_napl(k, carry):
        send_tile(0, lax.rem(n + k, chunks))
        return carry

    still = (zero,) * Z
    lax.fori_loop(0, width // B, functools.partial(inner_flux, 0), still, unroll=4)
    for side in range(2):
        await_open(side, conc_edge(0, side, 0))
    pl.when(first)(lambda: each_block(inlet_vel))
    pl.when(last)(lambda: each_block(outlet_vel))
    lax.fori_loop(0, chunks, first_transport, 0)
    lax.fori_loop(0, chunks, send_napl, 0)
    outlet_conc(1)
    lax.fori_loop(0, width // B, functools.partial(inner_flux, 1), still, unroll=4)
    lax.fori_loop(0, chunks, second_transport, 0)

    def settle_part(k, carry):
        for side in range(2):
            for s in (STEPS - 2, STEPS - 1):
                edge(s, side, k).wait_send()
        return carry

    def settle(k, carry):
        for side in range(2):
            sent_open(side, vel_edge(side, k))
            sent_open(side, conc_edge(1, side, k))
        return carry

    lax.fori_loop(0, parts, settle_part, 0)
    lax.fori_loop(0, chunks, settle, 0)
    for side in range(2):
        sent_open(side, poro_edge(side))
        sent_open(side, conc_edge(0, side, 0))

    def settle_tile(k, carry):
        @pl.when(k != n)
        def _():
            for a in range(2):
                to_tile(a, k).wait_send()
                from_tile(a, k).wait_recv()

        return carry

    lax.fori_loop(0, chunks, settle_tile, 0)
    for a in range(2):
        own_tile(a).wait()


def local(wide, narrow, populations, phase, porosity, napl, concentration, flags):
    width = phase.shape[2]
    tile = width // narrow
    padded = width + 2 * B
    f32 = jnp.float32
    DMA = pltpu.SemaphoreType.DMA

    def full():
        return pltpu.VMEM((Z, R, width), f32)

    any_space = pl.BlockSpec(memory_space=pl.ANY)
    scratch = [
        pltpu.VMEM((19, Z, R, width), f32),
        pltpu.VMEM((Z, R, width), jnp.int32),
        pltpu.VMEM((Z, R, padded), f32),
        full(),
        pltpu.VMEM((Z, R, padded), f32), pltpu.VMEM((Z, R, padded), f32),
        full(), full(), full(), full(),
        pltpu.VMEM((2, Z, width), jnp.int32),
        pltpu.VMEM((19, Z, R, padded), f32), pltpu.VMEM((19, Z, R, padded), f32),
        pltpu.VMEM((STEPS, 5, Z, R, padded), f32),
        pltpu.VMEM((STEPS, 5, Z, R, padded), f32),
        full(), full(),
        pltpu.VMEM((2, Z, R, width), f32), pltpu.VMEM((2, Z, R, width), f32),
        full(), full(),
        full(), pltpu.VMEM((Z, R, padded), f32), full(),
        full(), full(), full(), full(),
        full(), full(), full(), full(),
        full(),
        DMA((narrow,)), DMA((5,)), DMA((2,)),
        DMA((STEPS, 2, PARTS)), DMA((STEPS, 2, PARTS)),
        DMA((2,)), DMA((2,)),
        DMA((2, 2, narrow)), DMA((2, 2, narrow)),
        DMA((2, narrow)), DMA((2, narrow)),
        DMA((2, narrow)), DMA((2, narrow)),
    ]
    tiles = jax.ShapeDtypeStruct((Z, R * narrow, tile), f32)
    return pl.pallas_call(
        functools.partial(body, wide, narrow, width, tile),
        out_shape=(pltpu.VMEM(populations.shape, f32),) + (pltpu.VMEM(tiles.shape, f32),) * 2,
        in_specs=[any_space] * 6,
        out_specs=(pl.BlockSpec(memory_space=pltpu.VMEM),) * 3,
        scratch_shapes=scratch,
        compiler_params=pltpu.CompilerParams(
            collective_id=0, has_side_effects=True, vmem_limit_bytes=56 * 2**20
        ),
        name="dissolution",
    )(populations, phase, porosity, napl, concentration, flags)


def solution(mesh):
    strips = ("wide", "narrow")
    in_specs = (
        P(None, None, strips, None),
        P(None, strips, None),
        P(None, strips, None),
        P(None, strips, None),
        P(None, strips, None),
        P(),
    )
    out_specs = (
        P(None, None, strips, None),
        P(None, "wide", "narrow"),
        P(None, "wide", "narrow"),
    )
    fn = functools.partial(local, mesh.shape["wide"], mesh.shape["narrow"])
    return jax.shard_map(fn, mesh=mesh, in_specs=in_specs, out_specs=out_specs, check_vma=False)
```

```python
import functools

import jax
import jax.numpy as jnp
from jax import lax
from jax.experimental import pallas as pl
from jax.experimental.pallas import tpu as pltpu
from jax.sharding import PartitionSpec as P

MESH = pl.DeviceIdType.MESH
DIRS = [
    (0, 0, 0), (1, 0, 0), (-1, 0, 0), (0, 1, 0), (0, -1, 0), (0, 0, 1), (0, 0, -1),
    (1, 1, 0), (-1, -1, 0), (1, -1, 0), (-1, 1, 0), (1, 0, 1), (-1, 0, -1), (1, 0, -1), (-1, 0, 1),
    (0, 1, 1), (0, -1, -1), (0, 1, -1), (0, -1, 1),
]
OPP = [0, 2, 1, 4, 3, 6, 5, 8, 7, 10, 9, 12, 11, 14, 13, 16, 15, 18, 17]
UP = [1, 7, 9, 11, 13]
DOWN = [2, 8, 10, 12, 14]
ORDER = UP + DOWN + [0, 3, 4, 5, 6, 15, 16, 17, 18]
SLOT = {q: i for i, q in enumerate(ORDER)}
STEPS = 4
PARTS = 16
Z = 4
R = 8
B = 128


def collide(f, phase):
    total, diff = {}, {}
    for q in range(1, 19, 2):
        total[q] = f[q] + f[q + 1]
        diff[q] = f[q] - f[q + 1]
    rho = (
        ((f[0] + total[1]) + (total[3] + total[5]))
        + ((total[7] + total[9]) + (total[11] + total[13]))
        + (total[15] + total[17])
    )
    jx = (diff[1] + diff[7]) + (diff[9] + diff[11]) + diff[13]
    jy = (diff[3] + diff[7]) + (diff[15] - diff[9]) + diff[17]
    jz = (diff[5] + diff[11]) + (diff[15] - diff[13]) - diff[17]
    rho = jnp.where(phase == 2, jnp.nan, rho)
    factor = jnp.where(phase == 1, 0.5, 1.0)
    per = factor / rho
    vx, vy, vz = jx * per, jy * per, jz * per
    factor = factor * (3.75 / 36.0)
    nx, ny, nz = jx * factor, jy * factor, jz * factor
    hx, hy, hz = vx * 1.5, vy * 1.5, vz * 1.5
    sxx, syy, szz = nx * hx, ny * hy, nz * hz
    hx, hy = hx + hx, hy + hy
    xy, xz, yz = ny * hx, nz * hx, nz * hy
    even = rho * (1.25 / 36.0) - (sxx + syy + szz) * (1.0 / 3.0)
    post = [None] * 19
    post[0] = 12.0 * even - 0.25 * f[0]

    def pair(q, e, o):
        post[q] = (e + o) - 0.25 * f[q]
        post[q + 1] = (e - o) - 0.25 * f[q + 1]

    ex, ey, ez = even + sxx, even + syy, even + szz
    pair(1, ex + ex, nx + nx)
    pair(3, ey + ey, ny + ny)
    pair(5, ez + ez, nz + nz)
    exy, exz, eyz = ex + syy, ex + szz, ey + szz
    pair(7, exy + xy, nx + ny)
    pair(9, exy - xy, nx - ny)
    pair(11, exz + xz, nx + nz)
    pair(13, exz - xz, nx - nz)
    pair(15, eyz + yz, ny + nz)
    pair(17, eyz - yz, ny - nz)
    return post


def moments(f):
    total, diff = {}, {}
    for q in range(1, 19, 2):
        total[q] = f[q] + f[q + 1]
        diff[q] = f[q] - f[q + 1]
    rho = (
        ((f[0] + total[1]) + (total[3] + total[5]))
        + ((total[7] + total[9]) + (total[11] + total[13]))
        + (total[15] + total[17])
    )
    jx = (diff[1] + diff[7]) + (diff[9] + diff[11]) + diff[13]
    jy = (diff[3] + diff[7]) + (diff[15] - diff[9]) + diff[17]
    jz = (diff[5] + diff[11]) + (diff[15] - diff[13]) - diff[17]
    return rho, jx, jy, jz


def half_minmod(p, q):
    return 0.5 * jnp.maximum(jnp.minimum(p, q), jnp.minimum(jnp.maximum(p, q), 0.0))


def face_flux(back, here, ahead, far, w, a):
    step = ahead - here
    up = here + half_minmod(here - back, step)
    down = ahead - half_minmod(step, far - ahead)
    return a * jnp.where(a > 0, up, down) - (0.15 * w) * step


def body(
    wide, narrow, width, tile,
    pop_in, phase_in, poro_in, napl_in, conc_in, flags_in,
    pop_out, conc_out, napl_out,
    fbuf, phase, poro, napl, conc0, conc1, conc2, napl2, rate_buf, inner, flags, post0, post1, lo, hi,
    plo, phi, clo, chi, ulo, uhi, ux, uy, uz, wx, wl, wy, wz, ax, al, ay, az, inv,
    load_sem, small_sem, own_sem,
    send_sem, recv_sem, psend, precv, csend, crecv, usend, urecv, asend, arecv,
):
    posts, concs = (post0, post1), (conc0, conc1)
    w, n = lax.axis_index("wide"), lax.axis_index("narrow")
    chunks = narrow
    per_chunk = tile // B
    parts = PARTS
    part = width // parts
    strip = w * narrow + n

    def neighbour(offset):
        g = lax.rem(strip + offset + wide * narrow, wide * narrow)
        return (g // narrow, lax.rem(g, narrow))

    after, before = neighbour(1), neighbour(-1)
    first, last = strip == 0, strip == wide * narrow - 1

    barrier = pltpu.get_barrier_semaphore()
    pl.semaphore_signal(barrier, inc=1, device_id=after, device_id_type=MESH)
    pl.semaphore_signal(barrier, inc=1, device_id=before, device_id_type=MESH)
    for k in range(1, narrow):
        pl.semaphore_signal(
            barrier, inc=1, device_id=(w, lax.rem(n + k, narrow)), device_id_type=MESH
        )

    def part_cols(k):
        return pl.ds(pl.multiple_of(B + k * part, B), part)

    def cols(k):
        return pl.ds(pl.multiple_of(k * tile, tile), tile)

    def pcols(k):
        return pl.ds(pl.multiple_of(B + k * tile, B), tile)

    def load(k):
        return pltpu.make_async_copy(
            pop_in.at[:, :, :, cols(k)], fbuf.at[:, :, :, cols(k)], load_sem.at[k]
        )

    smalls = [
        pltpu.make_async_copy(phase_in, phase, small_sem.at[0]),
        pltpu.make_async_copy(poro_in, poro.at[:, :, pl.ds(B, width)], small_sem.at[1]),
        pltpu.make_async_copy(conc_in, conc0.at[:, :, pl.ds(B, width)], small_sem.at[2]),
        pltpu.make_async_copy(napl_in, napl, small_sem.at[3]),
        pltpu.make_async_copy(flags_in, flags, small_sem.at[4]),
    ]
    smalls[0].start()
    load(0).start()
    for k in range(1, chunks):
        load(k).start()
    for copy in smalls[1:]:
        copy.start()

    lane = lax.broadcasted_iota(jnp.int32, (R, B), 1)
    row = lax.broadcasted_iota(jnp.int32, (R, B), 0)
    nan = jnp.full((R, B), jnp.nan, jnp.float32)
    zero = jnp.zeros((R, B), jnp.float32)
    ends = (pl.ds(0, B), pl.ds(B + width, B))

    def fill(z, carry):
        for end in ends:
            for p in range(2):
                for q in range(19):
                    if DIRS[q][1]:
                        posts[p][SLOT[q], z, :, end] = nan
            for s in range(STEPS):
                for m in (1, 2):
                    lo[s, m, z, :, end] = nan
                    hi[s, m, z, :, end] = nan
            poro[z, :, end] = zero
            uy[z, :, end] = zero
            for p in range(2):
                concs[p][z, :, end] = zero
        return carry

    def edge(s, side, k):
        post = posts[s % 2]
        if side == 0:
            src = post.at[pl.ds(0, 5), :, pl.ds(R - 1, 1), part_cols(k)]
            dst = lo.at[s, :, :, pl.ds(R - 1, 1), part_cols(k)]
        else:
            src = post.at[pl.ds(5, 5), :, pl.ds(0, 1), part_cols(k)]
            dst = hi.at[s, :, :, pl.ds(0, 1), part_cols(k)]
        return pltpu.make_async_remote_copy(
            src_ref=src, dst_ref=dst, send_sem=send_sem.at[s, side, k], recv_sem=recv_sem.at[s, side, k],
            device_id=after if side == 0 else before, device_id_type=MESH,
        )

    def poro_edge(side):
        rows = pl.ds(R - 1, 1) if side == 0 else pl.ds(0, 1)
        inner = pl.ds(B, width)
        return pltpu.make_async_remote_copy(
            src_ref=poro.at[:, rows, inner], dst_ref=(plo if side == 0 else phi).at[:, rows, :],
            send_sem=psend.at[side], recv_sem=precv.at[side],
            device_id=after if side == 0 else before, device_id_type=MESH,
        )

    def conc_edge(p, side, k):
        rows = pl.ds(R - 2, 2) if side == 0 else pl.ds(0, 2)
        src, dst = (pl.ds(B, width), pl.ds(0, width)) if p == 0 else (pcols(k), cols(k))
        return pltpu.make_async_remote_copy(
            src_ref=concs[p].at[:, rows, src], dst_ref=(clo if side == 0 else chi).at[p, :, rows, dst],
            send_sem=csend.at[p, side, k], recv_sem=crecv.at[p, side, k],
            device_id=after if side == 0 else before, device_id_type=MESH,
        )

    def vel_edge(side, k):
        rows = pl.ds(R - 1, 1) if side == 0 else pl.ds(0, 1)
        return pltpu.make_async_remote_copy(
            src_ref=ux.at[:, rows, cols(k)], dst_ref=(ulo if side == 0 else uhi).at[:, rows, cols(k)],
            send_sem=usend.at[side, k], recv_sem=urecv.at[side, k],
            device_id=after if side == 0 else before, device_id_type=MESH,
        )

    def start_open(side, copy):
        pl.when(jnp.logical_not(last if side == 0 else first))(copy.start)

    def sent_open(side, copy):
        pl.when(jnp.logical_not(last if side == 0 else first))(copy.wait_send)

    def await_open(side, copy):
        pl.when(jnp.logical_not(first if side == 0 else last))(copy.wait_recv)

    def to_tile(a, k):
        src, dst = (napl2, napl_out) if a == 0 else (conc2, conc_out)
        rows = pl.ds(pl.multiple_of(n * R, R), R)
        return pltpu.make_async_remote_copy(
            src_ref=src.at[:, :, cols(k)], dst_ref=dst.at[:, rows, :],
            send_sem=asend.at[a, k], recv_sem=arecv.at[a, n], device_id=(w, k), device_id_type=MESH,
        )

    def from_tile(a, k):
        src, dst = (napl2, napl_out) if a == 0 else (conc2, conc_out)
        rows = pl.ds(pl.multiple_of(k * R, R), R)
        return pltpu.make_async_remote_copy(
            src_ref=src.at[:, :, cols(k)], dst_ref=dst.at[:, rows, :],
            send_sem=asend.at[a, k], recv_sem=arecv.at[a, k], device_id=(w, k), device_id_type=MESH,
        )

    def own_tile(a):
        src, dst = (napl2, napl_out) if a == 0 else (conc2, conc_out)
        rows = pl.ds(pl.multiple_of(n * R, R), R)
        return pltpu.make_async_copy(src.at[:, :, cols(n)], dst.at[:, rows, :], own_sem.at[a])

    def send_tile(a, k):
        @pl.when(k != n)
        def _():
            to_tile(a, k).start()

        @pl.when(k == n)
        def _():
            own_tile(a).start()

    def blocks(k, fn, carry=0, count=per_chunk):
        return lax.fori_loop(0, count, lambda i, c: fn(k * count + i, c), carry, unroll=True)

    def at(b):
        return pl.ds(pl.multiple_of(b * B, B), B)

    def start_block(b, carry):
        here, there = at(b), at(b + 1)
        for z in range(Z):
            f = [fbuf[q, z, :, here] for q in range(19)]
            out = collide(f, phase[z, :, here])
            for q in range(19):
                post0[SLOT[q], z, :, there] = out[q]
        return carry

    per_part, ratio = part // B, parts // chunks
    smalls[0].wait()
    load(0).wait()
    blocks(0, start_block, 0, per_part)
    pl.semaphore_wait(barrier, narrow + 1)
    for side in range(2):
        edge(0, side, 0).start()

    def first_part(k, carry):
        @pl.when(lax.rem(k, ratio) == 0)
        def _():
            load(k // ratio).wait()

        blocks(k, start_block, 0, per_part)
        for side in range(2):
            edge(0, side, k).start()
        return carry

    lax.fori_loop(1, parts, first_part, 0)
    lax.fori_loop(0, Z, fill, 0)
    for copy in smalls[1:]:
        copy.wait()
    def each_block(fn):
        def one(b, carry):
            for z in range(Z):
                fn(z, at(b), at(b + 1))
            return carry

        lax.fori_loop(0, width // B, one, 0)

    def inlet(z, here, there):
        plo[z, :, here] = jnp.broadcast_to(flags[0, z : z + 1, here].astype(jnp.float32), (R, B))
        for p in range(2):
            clo[p, z, :, here] = zero

    def outlet(z, here, there):
        phi[z, :, here] = jnp.broadcast_to(flags[1, z : z + 1, here].astype(jnp.float32), (R, B))

    def outlet_conc(p):
        def fill_rows(z, here, there):
            own = concs[p][z, :, there]
            chi[p, z, :, here] = jnp.where(row == 0, pltpu.roll(own, 1, 0), pltpu.roll(own, 2, 0))

        pl.when(last)(lambda: each_block(fill_rows))

    def inlet_vel(z, here, there):
        ulo[z, :, here] = pltpu.roll(ux[z, :, here], R - 1, 0)

    def outlet_vel(z, here, there):
        uhi[z, :, here] = pltpu.roll(ux[z, :, here], 1, 0)

    pl.when(first)(lambda: each_block(inlet))
    pl.when(last)(lambda: each_block(outlet))
    outlet_conc(0)
    for side in range(2):
        start_open(side, poro_edge(side))

    def stream(post, s, z, b):
        base = b * B + B

        def block(slot, layer, shift, ex):
            where = pl.ds(pl.multiple_of(base + shift, B), B)
            value = post[slot, layer, :, where]
            if ex == 1:
                value = jnp.where(row == R - 1, lo[s, slot, layer, :, where], value)
            elif ex == -1:
                value = jnp.where(row == 0, hi[s, slot - 5, layer, :, where], value)
            return value

        here = pl.ds(pl.multiple_of(base, B), B)
        f = []
        for q in range(19):
            ex, ey, ez = DIRS[q]
            slot, layer = SLOT[q], (z - ez) % Z
            if q == 0:
                f.append(post[slot, z, :, here])
                continue
            moved = block(slot, layer, 0, ex)
            if ey == 1:
                moved = pltpu.roll(jnp.where(lane == B - 1, block(slot, layer, -B, ex), moved), 1, 1)
            elif ey == -1:
                moved = pltpu.roll(jnp.where(lane == 0, block(slot, layer, B, ex), moved), B - 1, 1)
            if ex:
                moved = pltpu.roll(moved, 1 if ex == 1 else R - 1, 0)
            f.append(jnp.where(moved < jnp.inf, moved, post[SLOT[OPP[q]], z, :, here]))
        return f

    def await_edges(s, k):
        @pl.when(k == 0)
        def _():
            for side in range(2):
                edge(s, side, k).wait_recv()

        @pl.when(k < parts - 1)
        def _():
            for side in range(2):
                edge(s, side, k + 1).wait_recv()

    def one_step(s):
        old, new = posts[(s + 1) % 2], posts[s % 2]

        def move_block(b, c):
            for z in range(Z):
                out = collide(stream(old, s - 1, z, b), phase[z, :, at(b)])
                for q in range(19):
                    new[SLOT[q], z, :, at(b + 1)] = out[q]
            return c

        def chunk(k, c):
            await_edges(s - 1, k)

            if s >= 2:
                for side in range(2):
                    edge(s - 2, side, k).wait_send()

            blocks(k, move_block, 0, per_part)
            for side in range(2):
                edge(s, side, k).start()
            return c

        lax.fori_loop(0, parts, chunk, 0)

        if s == 1:
            for side in range(2):
                start_open(side, conc_edge(0, side, 0))
        if s == 2:
            for side in range(2):
                await_open(side, poro_edge(side))

            def coef(b, c):
                here, there, beyond = at(b), at(b + 1), at(b + 2)
                for z in range(Z):
                    own = poro[z, :, there]
                    high, low = phi[z, :, here], plo[z, :, here]
                    wx[z, :, here] = own * pltpu.roll(jnp.where(row == 0, high, own), R - 1, 0)
                    wl[z, :, here] = low * pltpu.roll(own, R - 1, 0)
                    wy[z, :, here] = own * pltpu.roll(jnp.where(lane == 0, poro[z, :, beyond], own), B - 1, 1)
                    wz[z, :, here] = own * poro[(z + 1) % Z, :, there]
                    inv[z, :, here] = 1.0 / jnp.maximum(own, 0.3)
                return c

            lax.fori_loop(0, width // B, coef, 0, unroll=2)

    for s in range(1, STEPS):
        one_step(s)

    def last_block(b, carry):
        here, there = at(b), at(b + 1)
        for z in range(Z):
            f = stream(posts[(STEPS - 1) % 2], STEPS - 1, z, b)
            solid = phase[z, :, here] == 2
            rho, jx, jy, jz = moments(f)
            per = jnp.where(solid, 0.0, 1.0) / jnp.where(solid, 1.0, rho)
            ux[z, :, here] = jnp.where(solid, 0.0, jx * per)
            uy[z, :, there] = jnp.where(solid, 0.0, jy * per)
            uz[z, :, here] = jnp.where(solid, 0.0, jz * per)
            for q in range(19):
                pop_out[q, z, :, here] = jnp.where(solid, fbuf[q, z, :, here], f[q])
        return carry

    def last_part(k, carry):
        await_edges(STEPS - 1, k)
        blocks(k, last_block, 0, per_part)

        @pl.when(lax.rem(k, ratio) == ratio - 1)
        def _():
            for side in range(2):
                start_open(side, vel_edge(side, k // ratio))

        return carry

    lax.fori_loop(0, parts, last_part, 0)

    def inner_flux(step, b, carry):
        here, there, back, beyond = at(b), at(b + 1), at(b), at(b + 2)
        conc = concs[step]
        c = [conc[z, :, there] for z in range(Z)]
        if step == 0:
            for z in range(Z):
                vy = uy[z, :, there]
                ay[z, :, here] = wy[z, :, here] * (
                    0.5 * (vy + pltpu.roll(jnp.where(lane == 0, uy[z, :, beyond], vy), B - 1, 1))
                )
                az[z, :, here] = wz[z, :, here] * (0.5 * (uz[z, :, here] + uz[(z + 1) % Z, :, here]))
        zflux = [
            face_flux(
                c[(z - 1) % Z], c[z], c[(z + 1) % Z], c[(z + 2) % Z], wz[z, :, here], az[z, :, here]
            )
            for z in range(Z)
        ]
        flow = []
        for z in range(Z):
            own = c[z]
            cb, cn = conc[z, :, back], conc[z, :, beyond]
            left = pltpu.roll(jnp.where(lane == B - 1, cb, own), 1, 1)
            right = pltpu.roll(jnp.where(lane == 0, cn, own), B - 1, 1)
            right2 = pltpu.roll(jnp.where(lane < 2, cn, own), B - 2, 1)
            yflux = face_flux(left, own, right, right2, wy[z, :, here], ay[z, :, here])
            flow.append(yflux)
            change = pltpu.roll(jnp.where(lane == B - 1, carry[z], yflux), 1, 1) - yflux
            inner[z, :, here] = change + (zflux[(z - 1) % Z] - zflux[z])
        return tuple(flow)

    def transport(step, b, carry):
        here, there = at(b), at(b + 1)
        conc = concs[step]
        for z in range(Z):
            own = conc[z, :, there]
            high = chi[step, z, :, here]
            low = clo[step, z, :, here]
            if step == 0:
                vx = ux[z, :, here]
                nxt = pltpu.roll(jnp.where(row == 0, uhi[z, :, here], vx), R - 1, 0)
                a = wx[z, :, here] * (0.5 * (vx + nxt))
                e = wl[z, :, here] * (0.5 * (ulo[z, :, here] + pltpu.roll(vx, R - 1, 0)))
                ax[z, :, here] = a
                al[z, :, here] = e
            else:
                a, e = ax[z, :, here], al[z, :, here]
            up1, up2 = pltpu.roll(own, R - 1, 0), pltpu.roll(own, R - 2, 0)
            down1 = pltpu.roll(jnp.where(row == R - 1, low, own), 1, 0)
            ahead = pltpu.roll(jnp.where(row == 0, high, own), R - 1, 0)
            far = pltpu.roll(jnp.where(row < 2, high, own), R - 2, 0)
            xflux = face_flux(down1, own, ahead, far, wx[z, :, here], a)
            xlow = face_flux(pltpu.roll(low, 1, 0), low, up1, up2, wl[z, :, here], e)
            change = pltpu.roll(jnp.where(row == R - 1, xlow, xflux), 1, 0) - xflux
            change = change + inner[z, :, here]
            if step == 0:
                s = napl[z, :, here]
                rate = 0.3 * s * (1.0 - own)
                new = own + (change + rate) * inv[z, :, here]
                conc1[z, :, there] = new
                s = s - 0.5 * rate
                rate = 0.3 * s * (1.0 - new)
                napl2[z, :, here] = s - 0.5 * rate
                rate_buf[z, :, here] = rate
            else:
                conc2[z, :, here] = own + (change + rate_buf[z, :, here]) * inv[z, :, here]
        return carry

    def first_transport(k, carry):
        for side in range(2):
            await_open(side, vel_edge(side, k))
        blocks(k, functools.partial(transport, 0))
        for side in range(2):
            start_open(side, conc_edge(1, side, k))
        return carry

    def second_transport(k, carry):
        for side in range(2):
            await_open(side, conc_edge(1, side, k))
        blocks(k, functools.partial(transport, 1))
        send_tile(1, k)
        return carry

    def send_napl(k, carry):
        send_tile(0, lax.rem(n + k, chunks))
        return carry

    still = (zero,) * Z
    lax.fori_loop(0, width // B, functools.partial(inner_flux, 0), still, unroll=4)
    for side in range(2):
        await_open(side, conc_edge(0, side, 0))
    pl.when(first)(lambda: each_block(inlet_vel))
    pl.when(last)(lambda: each_block(outlet_vel))
    lax.fori_loop(0, chunks, first_transport, 0, unroll=2)
    lax.fori_loop(0, chunks, send_napl, 0)
    outlet_conc(1)
    lax.fori_loop(0, width // B, functools.partial(inner_flux, 1), still, unroll=4)
    lax.fori_loop(0, chunks, second_transport, 0, unroll=2)

    def settle_part(k, carry):
        for side in range(2):
            for s in (STEPS - 2, STEPS - 1):
                edge(s, side, k).wait_send()
        return carry

    def settle(k, carry):
        for side in range(2):
            sent_open(side, vel_edge(side, k))
            sent_open(side, conc_edge(1, side, k))
        return carry

    lax.fori_loop(0, parts, settle_part, 0)
    lax.fori_loop(0, chunks, settle, 0)
    for side in range(2):
        sent_open(side, poro_edge(side))
        sent_open(side, conc_edge(0, side, 0))

    def settle_tile(k, carry):
        @pl.when(k != n)
        def _():
            for a in range(2):
                to_tile(a, k).wait_send()
                from_tile(a, k).wait_recv()

        return carry

    lax.fori_loop(0, chunks, settle_tile, 0)
    for a in range(2):
        own_tile(a).wait()


def local(wide, narrow, populations, phase, porosity, napl, concentration, flags):
    width = phase.shape[2]
    tile = width // narrow
    padded = width + 2 * B
    f32 = jnp.float32
    DMA = pltpu.SemaphoreType.DMA

    def full():
        return pltpu.VMEM((Z, R, width), f32)

    any_space = pl.BlockSpec(memory_space=pl.ANY)
    scratch = [
        pltpu.VMEM((19, Z, R, width), f32),
        pltpu.VMEM((Z, R, width), jnp.int32),
        pltpu.VMEM((Z, R, padded), f32),
        full(),
        pltpu.VMEM((Z, R, padded), f32), pltpu.VMEM((Z, R, padded), f32),
        full(), full(), full(), full(),
        pltpu.VMEM((2, Z, width), jnp.int32),
        pltpu.VMEM((19, Z, R, padded), f32), pltpu.VMEM((19, Z, R, padded), f32),
        pltpu.VMEM((STEPS, 5, Z, R, padded), f32),
        pltpu.VMEM((STEPS, 5, Z, R, padded), f32),
        full(), full(),
        pltpu.VMEM((2, Z, R, width), f32), pltpu.VMEM((2, Z, R, width), f32),
        full(), full(),
        full(), pltpu.VMEM((Z, R, padded), f32), full(),
        full(), full(), full(), full(),
        full(), full(), full(), full(),
        full(),
        DMA((narrow,)), DMA((5,)), DMA((2,)),
        DMA((STEPS, 2, PARTS)), DMA((STEPS, 2, PARTS)),
        DMA((2,)), DMA((2,)),
        DMA((2, 2, narrow)), DMA((2, 2, narrow)),
        DMA((2, narrow)), DMA((2, narrow)),
        DMA((2, narrow)), DMA((2, narrow)),
    ]
    tiles = jax.ShapeDtypeStruct((Z, R * narrow, tile), f32)
    return pl.pallas_call(
        functools.partial(body, wide, narrow, width, tile),
        out_shape=(pltpu.VMEM(populations.shape, f32),) + (pltpu.VMEM(tiles.shape, f32),) * 2,
        in_specs=[any_space] * 6,
        out_specs=(pl.BlockSpec(memory_space=pltpu.VMEM),) * 3,
        scratch_shapes=scratch,
        compiler_params=pltpu.CompilerParams(
            collective_id=0, has_side_effects=True, vmem_limit_bytes=56 * 2**20
        ),
        name="dissolution",
    )(populations, phase, porosity, napl, concentration, flags)


def solution(mesh):
    strips = ("wide", "narrow")
    in_specs = (
        P(None, None, strips, None),
        P(None, strips, None),
        P(None, strips, None),
        P(None, strips, None),
        P(None, strips, None),
        P(),
    )
    out_specs = (
        P(None, None, strips, None),
        P(None, "wide", "narrow"),
        P(None, "wide", "narrow"),
    )
    fn = functools.partial(local, mesh.shape["wide"], mesh.shape["narrow"])
    return jax.shard_map(fn, mesh=mesh, in_specs=in_specs, out_specs=out_specs, check_vma=False)
```
